128 devices in a mesh: ctx: 32 (over y, z, core), tp: 4 (over x).
Axes of the slice: x: 4, y: 4, z: 4, core: 2. Of those that a mesh axis runs over, the one named last changes fastest.
Arguments:
- query_short: bfloat16 [4096, 8192], P('ctx', 'tp'), may hold values from -6 to 6
- key_short: bfloat16 [4096, 8192], P('ctx', 'tp'), may hold values from -6 to 6
- value_short: bfloat16 [4096, 8192], P('ctx', 'tp'), may hold values from -6 to 6
- filter_short: bfloat16 [128, 8192], P(None, 'tp'), may hold values from -0.5 to 0.5
- norm_gain: float32 [8192], P('tp'), may hold values from 0.5 to 1.5
- key_long: bfloat16 [4096, 8192], P('ctx', 'tp'), may hold values from -6 to 6
- query_long: bfloat16 [4096, 8192], P('ctx', 'tp'), may hold values from -6 to 6
- filter_long: bfloat16 [4096, 8192], P('ctx', 'tp'), may hold values from -0.09375 to 0.09375
- out_adjoint: bfloat16 [4096, 8192], P('ctx', 'tp'), may hold values from -6 to 6
- contig_lengths: int32 [64], replicated, may hold values from 1 to 512, 4096 in all
Outputs:
- query_short_adjoint: bfloat16 [4096, 8192], P('ctx', 'tp')
- key_short_adjoint: bfloat16 [4096, 8192], P('ctx', 'tp')
- value_short_adjoint: bfloat16 [4096, 8192], P('ctx', 'tp')
- filter_short_adjoint: float32 [128, 8192], P(None, 'tp')
- gain_adjoint: float32 [8192], P('tp')
- key_long_adjoint: bfloat16 [4096, 8192], P('ctx', 'tp')
- query_long_adjoint: bfloat16 [4096, 8192], P('ctx', 'tp')
- filter_long_adjoint: bfloat16 [4096, 8192], P('ctx', 'tp')
The draws below stay inside these ranges and needn't reach their ends.
Inputs may be any that keep to these rules, and one draw needn't show every extreme that they name: `contig_lengths`: the lengths sum to 4096; the longest is exactly 512.
All inputs are finite; a program needn't handle non-finite values.
Results may differ from the reference program's by a relative error of at most 0.025.
Values may be sent and summed in bfloat16 or wider, within the bound.
A program may use at most 128 MiB of HBM per device.

```python
import math
import jax
import jax.numpy as jnp
import numpy as np
from jax import lax

D = 8192
FILT = 128
NCONTIG = 64
TOKENS = 4096


def levels(own_key, shape, split, low, high):
    loudness, own = 1.0, jax.random.fold_in(own_key, 6)
    for dim, shards_of in split:
        steps = jnp.exp(jax.random.uniform(jax.random.fold_in(own, dim), (shards_of,), jnp.float32, low / len(split), high / len(split)))
        loudness = loudness * jnp.repeat(steps, shape[dim] // shards_of).reshape([-1 if axis == dim else 1 for axis in range(len(shape))])
    return loudness


def profile(number_of, total, bound, skew):
    weights = [(1 << 20) // math.isqrt(grade ** skew) + 1 for grade in range(2, number_of + 1)]
    surplus, given = total - bound - (number_of - 1), [1] * (number_of - 1)
    while surplus > 0:
        free = [i for i in range(number_of - 1) if given[i] < bound]
        mass, remaining = sum([weights[i] for i in free]), surplus
        for i in free:
            more = min(bound - given[i], max(1, remaining * weights[i] // mass), surplus)
            given[i] = given[i] + more
            surplus = surplus - more
    return np.array([bound] + given)


def uneven_parts(stream_key, amount, total, limit, slope):
    if amount == 2:
        one = jax.random.randint(stream_key, (), max(1, total - limit), min(limit, total - 1) + 1)
        return jnp.stack([one, total - one])
    sizes = jnp.asarray(profile(amount, total, limit, slope), jnp.int32)
    twos = (amount - 1) // 2
    donor, taker = sizes[1:1 + 2 * twos:2], sizes[2:2 + 2 * twos:2]
    margin = jnp.minimum(donor - 1, limit - taker)
    moved = jax.random.randint(jax.random.fold_in(stream_key, 1), (twos,), 0, 1 << 20) % (margin + 1)
    sizes = sizes.at[1:1 + 2 * twos:2].set(donor - moved).at[2:2 + 2 * twos:2].set(taker + moved)
    return sizes[jax.random.permutation(jax.random.fold_in(stream_key, 2), amount)]


def centred(stream_key, dims, scale, reach, pieces=(), held_as=jnp.bfloat16):
    result = scale * jax.random.normal(stream_key, dims, jnp.float32)
    if pieces:
        result = result * levels(stream_key, dims, pieces, -0.22, 0.18)
    return jnp.clip(result, -reach, reach).astype(held_as)


def setup_inputs(seed: int = 0) -> dict:
    arg_keys = jax.random.split(jax.random.key(seed), 11)
    query_short = centred(arg_keys[0], (TOKENS, D), 1.0, 6.0, ((0, 32), (1, 4)))
    key_short = centred(arg_keys[1], (TOKENS, D), 1.0, 6.0, ((0, 32), (1, 4)))
    value_short = centred(arg_keys[2], (TOKENS, D), 1.0, 6.0, ((0, 32), (1, 4)))
    filter_short = centred(arg_keys[3], (FILT, D), FILT ** -0.5, 0.5, ((1, 4),))
    norm_gain = jnp.clip(1.0 + 0.1 * jax.random.normal(arg_keys[4], (D,), jnp.float32), 0.5, 1.5)
    key_long = centred(arg_keys[5], (TOKENS, D), 1.0, 6.0, ((0, 32), (1, 4)))
    query_long = centred(arg_keys[6], (TOKENS, D), 1.0, 6.0, ((0, 32), (1, 4)))
    filter_long = centred(arg_keys[7], (TOKENS, D), TOKENS ** -0.5, 0.09375, ((0, 32), (1, 4)))
    out_adjoint = centred(arg_keys[8], (TOKENS, D), 1.0, 6.0, ((0, 32), (1, 4)))
    contig_lengths = uneven_parts(arg_keys[9], NCONTIG, TOKENS, TOKENS // 8, 2).astype(jnp.int32)
    return dict(query_short=query_short, key_short=key_short, value_short=value_short, filter_short=filter_short, norm_gain=norm_gain, key_long=key_long, query_long=query_long, filter_long=filter_long, out_adjoint=out_adjoint, contig_lengths=contig_lengths)


EPS = 1e-06

def contig_ids(lengths, positions):
    starts = (jnp.cumsum(lengths) - lengths).astype(jnp.int32)
    return lax.optimization_barrier(jnp.sum((positions[:, None] >= starts[None, 1:]).astype(jnp.int32), axis=1)).astype(jnp.int32)

def short_conv(product, filt, labels):
    taps = filt.shape[0]
    length = product.shape[0]
    padded = jnp.concatenate([jnp.zeros((taps - 1, product.shape[1]), product.dtype), product], axis=0)
    pad_ids = jnp.concatenate([jnp.full((taps - 1,), -1, jnp.int32), labels])

    def step(lag, total):
        start = taps - 1 - lag
        piece = lax.dynamic_slice_in_dim(padded, start, length, 0)
        same = lax.dynamic_slice_in_dim(pad_ids, start, length, 0) == labels
        tap = lax.dynamic_index_in_dim(filt, lag, 0, keepdims=False)
        return total + jnp.where(same[:, None], piece.astype(jnp.float32) * tap.astype(jnp.float32)[None, :], jnp.float32(0.0))
    return lax.fori_loop(0, taps, step, jnp.zeros(product.shape, jnp.float32))

def short_conv_adjoint(mixed_adj, filt, labels):
    taps = filt.shape[0]
    length = mixed_adj.shape[0]
    padded = jnp.concatenate([mixed_adj, jnp.zeros((taps - 1, mixed_adj.shape[1]), mixed_adj.dtype)], axis=0)
    pad_ids = jnp.concatenate([labels, jnp.full((taps - 1,), -1, jnp.int32)])

    def step(lag, total):
        piece = lax.dynamic_slice_in_dim(padded, lag, length, 0)
        same = lax.dynamic_slice_in_dim(pad_ids, lag, length, 0) == labels
        tap = lax.dynamic_index_in_dim(filt, lag, 0, keepdims=False)
        return total + jnp.where(same[:, None], piece.astype(jnp.float32) * tap.astype(jnp.float32)[None, :], jnp.float32(0.0))
    return lax.fori_loop(0, taps, step, jnp.zeros(mixed_adj.shape, jnp.float32))

def short_filter_adjoint(product, mixed_adj, labels, taps):
    length = product.shape[0]
    padded = jnp.concatenate([jnp.zeros((taps - 1, product.shape[1]), product.dtype), product], axis=0)
    pad_ids = jnp.concatenate([jnp.full((taps - 1,), -1, jnp.int32), labels])

    def step(lag, carry):
        start = taps - 1 - lag
        piece = lax.dynamic_slice_in_dim(padded, start, length, 0)
        same = lax.dynamic_slice_in_dim(pad_ids, start, length, 0) == labels
        row = lax.optimization_barrier(jnp.sum(jnp.where(same[:, None], piece.astype(jnp.float32) * mixed_adj.astype(jnp.float32), jnp.float32(0.0)), axis=0))
        return lax.dynamic_update_index_in_dim(carry, row, lag, 0)
    return lax.fori_loop(0, taps, step, jnp.zeros((taps, product.shape[1]), jnp.float32))

def long_conv(filt, signal):
    length = filt.shape[0]
    size = 2 * length
    spectrum = jnp.fft.rfft(filt.astype(jnp.float32), n=size, axis=0) * jnp.fft.rfft(signal.astype(jnp.float32), n=size, axis=0)
    return jnp.fft.irfft(spectrum, n=size, axis=0)[:length]

def reference(query_short, key_short, value_short, filter_short, norm_gain, key_long, query_long, filter_long, out_adjoint, contig_lengths):
    f32 = jnp.float32
    bf16 = jnp.bfloat16
    labels = contig_ids(contig_lengths, jnp.arange(TOKENS, dtype=jnp.int32))
    product = (key_short.astype(f32) * value_short.astype(f32)).astype(bf16)
    mixed = short_conv(product, filter_short, labels)
    gated = query_short.astype(f32) * mixed
    scale = lax.rsqrt(lax.optimization_barrier(jnp.sum(gated * gated, axis=1)) / D + EPS)
    normed = gated * scale[:, None] * norm_gain[None, :]
    signal = (normed * key_long.astype(f32)).astype(bf16)
    upstream = (out_adjoint.astype(f32) * query_long.astype(f32)).astype(bf16)
    conv_out = long_conv(filter_long, signal).astype(bf16)
    flipped = jnp.flip(upstream, 0)
    signal_adj = jnp.flip(long_conv(filter_long, flipped), 0).astype(bf16)
    filter_long_adjoint = jnp.flip(long_conv(signal, flipped), 0).astype(bf16)
    query_long_adjoint = (out_adjoint.astype(f32) * conv_out.astype(f32)).astype(bf16)
    signal_f = signal_adj.astype(f32)
    key_long_adjoint = (signal_f * normed).astype(bf16)
    normed_adj = signal_f * key_long.astype(f32)
    gain_adjoint = lax.optimization_barrier(jnp.sum(normed_adj * gated * scale[:, None], axis=0))
    weighted = normed_adj * norm_gain[None, :]
    inner = lax.optimization_barrier(jnp.sum(weighted * gated, axis=1))
    gated_adj = scale[:, None] * weighted - gated * (scale * scale * scale * inner / D)[:, None]
    query_short_adjoint = (gated_adj * mixed).astype(bf16)
    mixed_adj = (gated_adj * query_short.astype(f32)).astype(bf16)
    product_adj = short_conv_adjoint(mixed_adj, filter_short, labels)
    filter_short_adjoint = short_filter_adjoint(product, mixed_adj, labels, filter_short.shape[0])
    key_short_adjoint = (product_adj * value_short.astype(f32)).astype(bf16)
    value_short_adjoint = (product_adj * key_short.astype(f32)).astype(bf16)
    return (query_short_adjoint, key_short_adjoint, value_short_adjoint, filter_short_adjoint, gain_adjoint, key_long_adjoint, query_long_adjoint, filter_long_adjoint)
```

```python
import math

import jax
import jax.numpy as jnp
import ml_dtypes
import numpy as np
from jax import lax
from jax.experimental import pallas as pl
from jax.experimental.pallas import tpu as pltpu
from jax.sharding import PartitionSpec as P

D = 8192
EPS = 1e-06
F32 = jnp.float32
BF16 = jnp.bfloat16
ROWS = 128
BLOCKS = 32
HALVES = (64, 32, 16, 8, 4, 2, 1)
PITCH = 264
VMEM = pl.BlockSpec(memory_space=pltpu.VMEM)


def odd_angles(size):
    return 2.0 * math.pi * (np.arange(size // 2) + 0.5) / size


def short_tables():
    into_re, into_im, taps_re, taps_im, out_re, out_im = ([] for _ in range(6))
    for half in (ROWS,) + HALVES:
        theta = odd_angles(2 * half)
        pairs = 1 if half == ROWS else ROWS // (2 * half)
        for pair in range(pairs):
            base = 0 if half == ROWS else pair * 2 * half
            first = np.zeros((half, ROWS)), np.zeros((half, ROWS))
            last = np.zeros((half, ROWS)), np.zeros((half, ROWS))
            taps = np.zeros((half, ROWS)), np.zeros((half, ROWS))
            ramp = np.arange(half)
            first[0][:, base : base + half] = np.cos(np.outer(theta, ramp))
            first[1][:, base : base + half] = -np.sin(np.outer(theta, ramp))
            start = 0 if half == ROWS else base + half
            last[0][:, start : start + half] = np.cos(np.outer(theta, ramp + half)) / half
            last[1][:, start : start + half] = -np.sin(np.outer(theta, ramp + half)) / half
            lags = np.arange(1, min(2 * half, ROWS))
            taps[0][:, lags] = np.cos(np.outer(theta, lags))
            taps[1][:, lags] = -np.sin(np.outer(theta, lags))
            for parts, pair_of in ((into_re, first), (out_re, last), (taps_re, taps)):
                parts.append(pair_of[0])
            for parts, pair_of in ((into_im, first), (out_im, last), (taps_im, taps)):
                parts.append(pair_of[1])

    def joined(re, im):
        re, im = np.concatenate(re), np.concatenate(im)
        return np.concatenate([re[:ROWS], im[:ROWS], re[ROWS:], im[ROWS:]]).astype(ml_dtypes.bfloat16)

    return joined(into_re, into_im), joined(taps_re, taps_im), joined(out_re, out_im)


def long_tables():
    theta = odd_angles(256)
    inner = np.outer(theta, np.arange(ROWS))
    into = np.concatenate([np.cos(inner), -np.sin(inner)])
    outer = np.outer(np.arange(256), theta)
    out = np.concatenate([np.cos(outer), -np.sin(outer)], axis=1) / 128.0
    angle = 2.0 * math.pi * (np.outer(np.arange(64), np.arange(BLOCKS)) % 64) / 64.0
    cos, sin = np.cos(angle), np.sin(angle)
    over = np.block([[cos, sin], [-sin, cos]])
    back = np.block([[cos.T, -sin.T], [sin.T, cos.T]]) / 64.0
    return [table.astype(ml_dtypes.bfloat16) for table in (into, over, back, out)]


def dot(a, b):
    return jnp.dot(a, b, preferred_element_type=F32)


def turned(x):
    return pltpu.roll(x, 64, 1)


def left(shape):
    return lax.broadcasted_iota(jnp.int32, shape, 1) < 64


def lanes(tile, width):
    return pl.ds(pl.multiple_of(tile * width, width), width)


def mask_rows(lengths, first):
    before = lax.broadcasted_iota(jnp.int32, (64, 64), 1) < lax.broadcasted_iota(
        jnp.int32, (64, 64), 0
    )
    starts = jnp.sum(jnp.where(before, lengths, 0), axis=1, keepdims=True)
    later = lax.broadcasted_iota(jnp.int32, (64, ROWS), 0) >= 1

    def label(positions):
        return jnp.sum(
            jnp.where(later & (positions + first >= starts), 1, 0), axis=0, keepdims=True
        )

    own = lax.broadcasted_iota(jnp.int32, (1, ROWS), 1)
    here = label(own)
    before_here = label(own - own - 1)
    last_here = label(own - own + (ROWS - 1))

    def same(a, b):
        return (a == b).astype(F32)

    halves = [same(here, label((own // (2 * half)) * (2 * half) + half - 1)) for half in HALVES]
    return dict(
        halves=halves,
        halo_own=same(here, before_here),
        halo_before=same(label(own - ROWS), before_here),
        next_own=same(here, last_here),
        next_after=same(label(own + ROWS), last_here),
    )


def spread(masks, head):
    parts = [jnp.broadcast_to(masks[head], (256, ROWS))]
    for _ in range(2):
        parts += [jnp.broadcast_to(mask, (64, ROWS)) for mask in masks["halves"]]
    return jnp.concatenate(parts, axis=0)


def masked(table, masks, head):
    return (table.astype(F32) * spread(masks, head)).astype(BF16)


H = 448


def complex_product(a, b):
    return a[0] * b[0] - a[1] * b[1], a[0] * b[1] + a[1] * b[0]


def adjoint_product(a, b):
    return a[0] * b[0] + a[1] * b[1], a[1] * b[0] - a[0] * b[1]


def split_spectrum(table, head_rows, body_rows):
    head = dot(table[0:256, :], head_rows)
    body = dot(table[256:, :], body_rows)
    return (head[:128], head[128:]), (body[:H], body[H:])


def rejoined(head, body):
    return jnp.concatenate([head[0], head[1], body[0], body[1]], axis=0).astype(BF16)


def prep_kernel(ks, vs, oa, ql, fl, product, pairs):
    def step(tile, carry):
        at = lanes(tile, 128)
        product[:, at] = (ks[:, at].astype(F32) * vs[:, at].astype(F32)).astype(BF16)
        up = oa[:, at].astype(F32) * ql[:, at].astype(F32)
        taps = fl[:, at].astype(F32)
        side = left((ROWS, 128))
        pairs[2 * tile] = jnp.where(side, taps, turned(up)).astype(BF16)
        pairs[2 * tile + 1] = jnp.where(side, turned(taps), up).astype(BF16)
        return carry

    lax.fori_loop(0, 16, step, 0)


def short_kernel(qs, product, halo, fs, lengths, into, taps, out, mixed, power, into_m, out_m):
    first = lax.axis_index("ctx") * ROWS
    masks = mask_rows(lengths[...], first)
    into_m[...] = masked(into[...], masks, "halo_before")
    out_m[...] = masked(out[...], masks, "halo_own").astype(F32).T.astype(BF16)

    def step(tile, total):
        at = lanes(tile, 256)
        x = product[:, at]
        f = fs[:, at]
        x_head, x_body = split_spectrum(into_m, halo[:, at], x)
        f_head, f_body = split_spectrum(taps, f, f)
        q = rejoined(complex_product(x_head, f_head), complex_product(x_body, f_body))
        y = dot(out_m[...], q) + x.astype(F32) * f[0:1, :].astype(F32)
        mixed[:, at] = y
        gated = qs[:, at].astype(F32) * y
        return total + jnp.sum(gated * gated, axis=1, keepdims=True)

    total = lax.fori_loop(0, 8, step, jnp.zeros((ROWS, 1), F32))
    power[...] = jnp.broadcast_to(total, (ROWS, 128))


def signal_kernel(qs, mixed, power, gain, kl, packed):
    scale = lax.rsqrt(power[...] / D + EPS)

    def step(tile, carry):
        at = lanes(tile, 128)
        gated = qs[:, at].astype(F32) * mixed[:, at]
        normed = gated * scale * gain[:, at]
        s = normed * kl[:, at].astype(F32)
        side = left((64, 128))
        low, high = s[:64], s[64:]
        packed[2 * tile] = jnp.where(side, low, turned(high)).astype(BF16)
        packed[2 * tile + 1] = jnp.where(side, turned(low), high).astype(BF16)
        return carry

    lax.fori_loop(0, 16, step, 0)


def inner_transform(read, into, spec):
    def step(j, carry):
        both = dot(into[...], jnp.concatenate([read(2 * j), read(2 * j + 1)], axis=1))
        spec[pl.ds(2 * j * PITCH, 256), :] = both[:, :128]
        spec[pl.ds((2 * j + 1) * PITCH, 256), :] = both[:, 128:]
        return carry

    lax.fori_loop(0, BLOCKS // 2, step, 0)


GROUP = 4


def outer_transform(group, over, spec):
    columns = []
    for member in range(GROUP):
        f = group * GROUP + member
        columns.append(
            jnp.concatenate(
                [
                    spec[pl.ds(f, BLOCKS, stride=PITCH), :],
                    spec[pl.ds(f + 128, BLOCKS, stride=PITCH), :],
                ],
                axis=0,
            )
        )
    return dot(over[...], jnp.concatenate(columns, axis=1).astype(BF16))


def outer_inverse(group, value, back, spec):
    result = dot(back[...], value)
    for member in range(GROUP):
        f = group * GROUP + member
        piece = result[:, 128 * member : 128 * (member + 1)]
        spec[pl.ds(f, BLOCKS, stride=PITCH), :] = piece[:BLOCKS]
        spec[pl.ds(f + 128, BLOCKS, stride=PITCH), :] = piece[BLOCKS:]


def inner_inverse(out, spec, result):
    def step(j, carry):
        both = jnp.concatenate(
            [spec[pl.ds(2 * j * PITCH, 256), :], spec[pl.ds((2 * j + 1) * PITCH, 256), :]], axis=1
        )
        value = dot(out[...], both.astype(BF16))
        result[2 * j] = value[:, :128]
        result[2 * j + 1] = value[:, 128:]
        return carry

    lax.fori_loop(0, BLOCKS // 2, step, 0)


def group_lanes():
    return (lax.broadcasted_iota(jnp.int32, (64, 128 * GROUP), 1) & 127) < 64


def group_turned(x):
    return jnp.concatenate(
        [turned(x[:, 128 * m : 128 * (m + 1)]) for m in range(GROUP)], axis=1
    )


def long_kernel(pairs, packed, into, over, back, out, joined, adjoint, spec, spec_b, held, result):
    inner_transform(lambda j: pairs[j], into, spec)

    def early(group, carry):
        z = outer_transform(group, over, spec)
        held[:, lanes(group, 128 * GROUP)] = z
        zr, zi = z[:64], z[64:]
        ur, ui = group_turned(zr), group_turned(zi)
        side = group_lanes()
        zi_s = jnp.where(side, zi, -zi)
        ui_s = jnp.where(side, ui, -ui)
        re = zr * ur + zi * ui
        im = ui_s * zr + ur * (-zi_s)
        outer_inverse(group, jnp.concatenate([re, im], axis=0).astype(BF16), back, spec_b)
        return carry

    lax.fori_loop(0, 128 // GROUP, early, 0)
    inner_inverse(out, spec_b, result)

    def early_out(j, carry):
        now = result[j]
        later = result[jnp.minimum(j + 1, BLOCKS - 1)]
        tail = jnp.where(j < BLOCKS - 1, later[128:], 0.0)
        value = now[:128] - tail
        adjoint[j] = jnp.where(left((64, 128)), value[:64], value[64:]).astype(BF16)
        return carry

    lax.fori_loop(0, BLOCKS, early_out, 0)

    def both_halves(j):
        p = packed[j].astype(F32)
        r = turned(p)
        side = left((64, 128))
        return jnp.concatenate([jnp.where(side, p, r), jnp.where(side, r, p)], axis=0).astype(BF16)

    inner_transform(both_halves, into, spec)

    def late(group, carry):
        s = outer_transform(group, over, spec)
        z = held[:, lanes(group, 128 * GROUP)]
        zr, zi = z[:64], z[64:]
        sr, si = s[:64], s[64:]
        si = jnp.where(group_lanes(), si, -si)
        re = zr * sr - zi * si
        im = zi * sr + zr * si
        outer_inverse(group, jnp.concatenate([re, im], axis=0).astype(BF16), back, spec_b)
        return carry

    lax.fori_loop(0, 128 // GROUP, late, 0)
    inner_inverse(out, spec_b, result)

    def late_out(j, carry):
        now = result[j]
        before = jnp.where(j > 0, result[jnp.maximum(j - 1, 0)][128:], 0.0)
        later = jnp.where(j < BLOCKS - 1, result[jnp.minimum(j + 1, BLOCKS - 1)][128:], 0.0)
        joined[j] = (now[:128] + jnp.where(left((ROWS, 128)), before, -later)).astype(BF16)
        return carry

    lax.fori_loop(0, BLOCKS, late_out, 0)


def finish_long_kernel(joined, oa, ql_adj, fl_adj):
    def step(tile, carry):
        at = lanes(tile, 128)
        even, odd = joined[2 * tile].astype(F32), joined[2 * tile + 1].astype(F32)
        side = left((ROWS, 128))
        conv = jnp.where(side, even, turned(odd))
        ql_adj[:, at] = (oa[:, at].astype(F32) * conv).astype(BF16)
        fl_adj[:, at] = jnp.where(side, turned(even), odd).astype(BF16)
        return carry

    lax.fori_loop(0, 16, step, 0)


def unpacked(adjoint, tile):
    even, odd = adjoint[2 * tile].astype(F32), adjoint[2 * tile + 1].astype(F32)
    side = left((64, 128))
    return jnp.concatenate(
        [jnp.where(side, even, turned(odd)), jnp.where(side, turned(even), odd)], axis=0
    )


def inner_kernel(adjoint, qs, mixed, power, gain, kl, kl_adj, gain_part, inner):
    scale = lax.rsqrt(power[...] / D + EPS)

    def step(tile, total):
        at = lanes(tile, 128)
        signal_adj = unpacked(adjoint, tile)
        gated = qs[:, at].astype(F32) * mixed[:, at]
        normed = gated * scale * gain[:, at]
        kl_adj[:, at] = (signal_adj * normed).astype(BF16)
        normed_adj = signal_adj * kl[:, at].astype(F32)
        product = normed_adj * gated
        gain_part[:, at] = jnp.sum(product * scale, axis=0, keepdims=True)
        return total + jnp.sum(product * gain[:, at], axis=1, keepdims=True)

    total = lax.fori_loop(0, 16, step, jnp.zeros((ROWS, 1), F32))
    inner[...] = jnp.broadcast_to(total, (ROWS, 128))


def mixed_adj_kernel(adjoint, qs, mixed, power, inner, gain, kl, qs_adj, mixed_adj):
    scale = lax.rsqrt(power[...] / D + EPS)
    drop = scale * scale * scale * inner[...] / D

    def step(tile, carry):
        at = lanes(tile, 128)
        q = qs[:, at].astype(F32)
        y = mixed[:, at]
        weighted = unpacked(adjoint, tile) * kl[:, at].astype(F32) * gain[:, at]
        gated_adj = scale * weighted - q * y * drop
        qs_adj[:, at] = (gated_adj * y).astype(BF16)
        mixed_adj[:, at] = (gated_adj * q).astype(BF16)
        return carry

    lax.fori_loop(0, 16, step, 0)


def short_back_kernel(
    ks, vs, product, halo, mixed_adj, after, fs, lengths, into, taps, out, taps_t, into_t,
    ks_adj, vs_adj, fs_part, into_m, into_tm, out_m, next_m,
):
    first = lax.axis_index("ctx") * ROWS
    masks = mask_rows(lengths[...], first)
    into_m[...] = masked(into[...], masks, "halo_before")
    into_tm[...] = masked(into[...], masks, "next_own").astype(F32).T.astype(BF16)
    out_m[...] = masked(out[...], masks, "halo_own")
    next_m[...] = (out[0:256, :].astype(F32) * masks["next_after"]).astype(BF16)

    def step(tile, carry):
        at = lanes(tile, 256)
        x = product[:, at]
        f = fs[:, at]
        m = mixed_adj[:, at]
        x_head, x_body = split_spectrum(into_m, halo[:, at], x)
        f_head, f_body = split_spectrum(taps, f, f)
        m_head, m_body = split_spectrum(out_m, m, m)
        n = dot(next_m[...], after[:, at])
        n_head = (n[:128], n[128:])
        p = rejoined(adjoint_product(n_head, f_head), adjoint_product(m_body, f_body))
        g = rejoined(adjoint_product(m_head, x_head), adjoint_product(m_body, x_body))
        tap = f[0:1, :].astype(F32)
        wide = m.astype(F32)
        back = dot(into_tm[...], p) + wide * tap
        ks_adj[:, at] = (back * vs[:, at].astype(F32)).astype(BF16)
        vs_adj[:, at] = (back * ks[:, at].astype(F32)).astype(BF16)
        zero = jnp.sum(wide * x.astype(F32), axis=0, keepdims=True)
        row = lax.broadcasted_iota(jnp.int32, (ROWS, 256), 0)
        fs_part[:, at] = dot(taps_t[...], g) + jnp.where(row == 0, zero, 0.0)
        return carry

    lax.fori_loop(0, 8, step, 0)


def call(kernel, outs, scratch, *operands):
    return pl.pallas_call(
        kernel,
        out_shape=[jax.ShapeDtypeStruct(shape, dtype) for shape, dtype in outs],
        in_specs=[VMEM] * len(operands),
        out_specs=[VMEM] * len(outs),
        scratch_shapes=[pltpu.VMEM(shape, dtype) for shape, dtype in scratch],
        compiler_params=pltpu.CompilerParams(vmem_limit_bytes=56 * 1024 * 1024),
    )(*operands)


def shifted(block, distance):
    devices = range(BLOCKS)
    return lax.ppermute(
        block, "ctx", [(i - distance, i) for i in devices if i - distance in devices]
    )


def swapped(blocks):
    return lax.all_to_all(blocks, "ctx", split_axis=0, concat_axis=0, tiled=True)


def local(qs, ks, vs, fs, gain, kl, ql, fl, oa, contig_lengths):
    into, taps, out = (jnp.asarray(table) for table in short_tables())
    l_into, l_over, l_back, l_out = (jnp.asarray(table) for table in long_tables())
    gain = gain[None, :]
    lengths = contig_lengths[None, :]
    wide = ROWS, qs.shape[1]
    product, pairs = call(
        prep_kernel, [(wide, BF16), ((BLOCKS, ROWS, 128), BF16)], [], ks, vs, oa, ql, fl
    )
    halo = shifted(product, 1)
    pairs = swapped(pairs)
    table = (1152, ROWS)
    turned_table = (ROWS, 1152)
    mixed, power = call(
        short_kernel, [(wide, F32), ((ROWS, 128), F32)], [(table, BF16), (turned_table, BF16)],
        qs, product, halo, fs, lengths, into, taps, out,
    )
    power = lax.psum(power, "tp")
    (packed,) = call(
        signal_kernel, [((BLOCKS, 64, 128), BF16)], [], qs, mixed, power, gain, kl
    )
    packed = swapped(packed)
    spec = (BLOCKS * PITCH, 128)
    joined, adjoint = call(
        long_kernel,
        [((BLOCKS, ROWS, 128), BF16), ((BLOCKS, 64, 128), BF16)],
        [(spec, F32), (spec, F32), ((128, 128 * 128), F32), ((BLOCKS, 256, 128), F32)],
        pairs, packed, l_into, l_over, l_back, l_out,
    )
    adjoint = swapped(adjoint)
    joined = swapped(joined)
    ql_adj, fl_adj = call(finish_long_kernel, [(wide, BF16), (wide, BF16)], [], joined, oa)
    kl_adj, gain_part, inner = call(
        inner_kernel, [(wide, BF16), ((1, wide[1]), F32), ((ROWS, 128), F32)], [],
        adjoint, qs, mixed, power, gain, kl,
    )
    inner = lax.psum(inner, "tp")
    qs_adj, mixed_adj = call(
        mixed_adj_kernel, [(wide, BF16), (wide, BF16)], [],
        adjoint, qs, mixed, power, inner, gain, kl,
    )
    after = shifted(mixed_adj, -1)
    ks_adj, vs_adj, fs_part = call(
        short_back_kernel, [(wide, BF16), (wide, BF16), (wide, F32)],
        [(table, BF16), (turned_table, BF16), (table, BF16), ((256, ROWS), BF16)],
        ks, vs, product, halo, mixed_adj, after, fs, lengths, into, taps, out,
        taps.T, into.T,
    )
    pieces = swapped(fs_part.astype(BF16).reshape(BLOCKS, 4, wide[1]))
    piece = jnp.sum(pieces.astype(F32), axis=0).astype(BF16)
    fs_adj = lax.all_gather(piece, "ctx", axis=0, tiled=True).astype(F32)
    gain_adj = lax.psum(gain_part[0], "ctx")
    return qs_adj, ks_adj, vs_adj, fs_adj, gain_adj, kl_adj, ql_adj, fl_adj


def solution(mesh):
    spread_spec = P("ctx", "tp")
    in_specs = (
        spread_spec, spread_spec, spread_spec, P(None, "tp"), P("tp"),
        spread_spec, spread_spec, spread_spec, spread_spec, P(),
    )
    out_specs = (
        spread_spec, spread_spec, spread_spec, P(None, "tp"), P("tp"),
        spread_spec, spread_spec, spread_spec,
    )
    return jax.shard_map(local, mesh=mesh, in_specs=in_specs, out_specs=out_specs, check_vma=False)
```

```python
import math

import jax
import jax.numpy as jnp
import ml_dtypes
import numpy as np
from jax import lax
from jax.experimental import pallas as pl
from jax.experimental.pallas import tpu as pltpu
from jax.sharding import PartitionSpec as P

D = 8192
EPS = 1e-06
F32 = jnp.float32
BF16 = jnp.bfloat16
ROWS = 128
BLOCKS = 32
HALVES = (64, 32, 16, 8, 4, 2, 1)
PITCH = 264
VMEM = pl.BlockSpec(memory_space=pltpu.VMEM)


def odd_angles(size):
    return 2.0 * math.pi * (np.arange(size // 2) + 0.5) / size


def short_tables():
    into_re, into_im, taps_re, taps_im, out_re, out_im = ([] for _ in range(6))
    for half in (ROWS,) + HALVES:
        theta = odd_angles(2 * half)
        pairs = 1 if half == ROWS else ROWS // (2 * half)
        for pair in range(pairs):
            base = 0 if half == ROWS else pair * 2 * half
            first = np.zeros((half, ROWS)), np.zeros((half, ROWS))
            last = np.zeros((half, ROWS)), np.zeros((half, ROWS))
            taps = np.zeros((half, ROWS)), np.zeros((half, ROWS))
            ramp = np.arange(half)
            first[0][:, base : base + half] = np.cos(np.outer(theta, ramp))
            first[1][:, base : base + half] = -np.sin(np.outer(theta, ramp))
            start = 0 if half == ROWS else base + half
            last[0][:, start : start + half] = np.cos(np.outer(theta, ramp + half)) / half
            last[1][:, start : start + half] = -np.sin(np.outer(theta, ramp + half)) / half
            lags = np.arange(1, min(2 * half, ROWS))
            taps[0][:, lags] = np.cos(np.outer(theta, lags))
            taps[1][:, lags] = -np.sin(np.outer(theta, lags))
            for parts, pair_of in ((into_re, first), (out_re, last), (taps_re, taps)):
                parts.append(pair_of[0])
            for parts, pair_of in ((into_im, first), (out_im, last), (taps_im, taps)):
                parts.append(pair_of[1])

    def joined(re, im):
        re, im = np.concatenate(re), np.concatenate(im)
        return np.concatenate([re[:ROWS], im[:ROWS], re[ROWS:], im[ROWS:]]).astype(ml_dtypes.bfloat16)

    return joined(into_re, into_im), joined(taps_re, taps_im), joined(out_re, out_im)


def long_tables():
    theta = odd_angles(256)
    inner = np.outer(theta, np.arange(ROWS))
    into = np.concatenate([np.cos(inner), -np.sin(inner)])
    outer = np.outer(np.arange(256), theta)
    out = np.concatenate([np.cos(outer), -np.sin(outer)], axis=1) / 128.0
    angle = 2.0 * math.pi * (np.outer(np.arange(64), np.arange(BLOCKS)) % 64) / 64.0
    cos, sin = np.cos(angle), np.sin(angle)
    over = np.block([[cos, sin], [-sin, cos]])
    back = np.block([[cos.T, -sin.T], [sin.T, cos.T]]) / 64.0
    return [table.astype(ml_dtypes.bfloat16) for table in (into, over, back, out)]


def dot(a, b):
    return jnp.dot(a, b, preferred_element_type=F32)


def turned(x):
    return pltpu.roll(x, 64, 1)


def left(shape):
    return lax.broadcasted_iota(jnp.int32, shape, 1) < 64


def lanes(tile, width):
    return pl.ds(pl.multiple_of(tile * width, width), width)


def mask_rows(lengths, first):
    before = lax.broadcasted_iota(jnp.int32, (64, 64), 1) < lax.broadcasted_iota(
        jnp.int32, (64, 64), 0
    )
    starts = jnp.sum(jnp.where(before, lengths, 0), axis=1, keepdims=True)
    tokens = BLOCKS * ROWS

    def label(positions):
        place = positions + first
        begun = jnp.sum(jnp.where(place >= starts, 1, 0), axis=0, keepdims=True)
        return begun + jnp.where(place >= tokens, 1, 0)

    own = lax.broadcasted_iota(jnp.int32, (1, ROWS), 1)
    here = label(own)
    before_here = label(own - own - 1)
    last_here = label(own - own + (ROWS - 1))

    def same(a, b):
        return (a == b).astype(F32)

    halves = [same(here, label((own // (2 * half)) * (2 * half) + half - 1)) for half in HALVES]
    return dict(
        halves=halves,
        halo_own=same(here, before_here),
        halo_before=same(label(own - ROWS), before_here),
        next_own=same(here, last_here),
        next_after=same(label(own + ROWS), last_here),
    )


def spread(masks, head):
    parts = [jnp.broadcast_to(masks[head], (256, ROWS))]
    for _ in range(2):
        parts += [jnp.broadcast_to(mask, (64, ROWS)) for mask in masks["halves"]]
    return jnp.concatenate(parts, axis=0)


def masked(table, masks, head):
    return (table.astype(F32) * spread(masks, head)).astype(BF16)


H = 448


def complex_product(a, b):
    return a[0] * b[0] - a[1] * b[1], a[0] * b[1] + a[1] * b[0]


def adjoint_product(a, b):
    return a[0] * b[0] + a[1] * b[1], a[1] * b[0] - a[0] * b[1]


def split_spectrum(table, head_rows, body_rows):
    head = dot(table[0:256, :], head_rows)
    body = dot(table[256:, :], body_rows)
    return (head[:128], head[128:]), (body[:H], body[H:])


def rejoined(head, body):
    return jnp.concatenate([head[0], head[1], body[0], body[1]], axis=0).astype(BF16)


GROUP = 16
SPAN = 8
WIDE = 512
CHIPS = 16
MESH = pl.DeviceIdType.MESH


def inner_transform(read, into, spec):
    def step(j, carry):
        value = dot(into[...], jnp.concatenate([read(SPAN * j + i) for i in range(SPAN)], axis=1))
        for i in range(SPAN):
            spec[pl.ds((SPAN * j + i) * PITCH, 256), :] = value[:, 128 * i : 128 * (i + 1)]
        return carry

    lax.fori_loop(0, BLOCKS // SPAN, step, 0)


def outer_transform(group, over, spec):
    columns = []
    for member in range(GROUP):
        f = group * GROUP + member
        columns.append(
            jnp.concatenate(
                [
                    spec[pl.ds(f, BLOCKS, stride=PITCH), :],
                    spec[pl.ds(f + 128, BLOCKS, stride=PITCH), :],
                ],
                axis=0,
            )
        )
    return dot(over[...], jnp.concatenate(columns, axis=1).astype(BF16))


def outer_inverse(group, re, im, back, spec):
    result = dot(back[...], jnp.concatenate([re, im], axis=0).astype(BF16))
    for member in range(GROUP):
        f = group * GROUP + member
        piece = result[:, 128 * member : 128 * (member + 1)]
        spec[pl.ds(f, BLOCKS, stride=PITCH), :] = piece[:BLOCKS]
        spec[pl.ds(f + 128, BLOCKS, stride=PITCH), :] = piece[BLOCKS:]


def inner_inverse(out, spec, result):
    def step(j, carry):
        value = dot(
            out[...],
            jnp.concatenate(
                [spec[pl.ds((SPAN * j + i) * PITCH, 256), :].astype(BF16) for i in range(SPAN)],
                axis=1,
            ),
        )
        for i in range(SPAN):
            result[SPAN * j + i] = value[:, 128 * i : 128 * (i + 1)]
        return carry

    lax.fori_loop(0, BLOCKS // SPAN, step, 0)


def group_lanes():
    return (lax.broadcasted_iota(jnp.int32, (64, 128 * GROUP), 1) & 127) < 64


def group_turned(x):
    return jnp.concatenate(
        [turned(x[:, 128 * m : 128 * (m + 1)]) for m in range(GROUP)], axis=1
    )


def unpacked(adjoint, tile):
    even, odd = adjoint[2 * tile].astype(F32), adjoint[2 * tile + 1].astype(F32)
    side = left((64, 128))
    return jnp.concatenate(
        [jnp.where(side, even, turned(odd)), jnp.where(side, turned(even), odd)], axis=0
    )


def chip_at(me, step):
    chip = me // 2
    return (chip // 4 + step // 4) % 4 * 4 + (chip + step) % 4


def send_block(send, recv, sems, me, dest):
    @pl.when(dest != me)
    def _():
        pltpu.make_async_remote_copy(
            src_ref=send.at[dest],
            dst_ref=recv.at[me],
            send_sem=sems[0],
            recv_sem=sems[1],
            device_id={"ctx": dest},
            device_id_type=MESH,
        ).start()

    @pl.when(dest == me)
    def _():
        recv[me] = send[me]


def wait_blocks(buffer, sem, count):
    part = buffer.at[pl.ds(0, count)]
    pltpu.make_async_copy(part, part, sem).wait()


def neighbour_copy(source, target, sems, dest):
    return pltpu.make_async_remote_copy(
        src_ref=source,
        dst_ref=target,
        send_sem=sems[0],
        recv_sem=sems[1],
        device_id={"ctx": dest},
        device_id_type=MESH,
    )


def send_sums(column, buffer, sems, col):
    buffer[col] = jnp.broadcast_to(column, (ROWS, 128)).T[:8]
    for step in range(1, 4):
        pltpu.make_async_remote_copy(
            src_ref=buffer.at[col],
            dst_ref=buffer.at[col],
            send_sem=sems[0],
            recv_sem=sems[1],
            device_id={"tp": (col + step) % 4},
            device_id_type=MESH,
        ).start()


def take_sums(buffer, sems):
    wait_blocks(buffer, sems[1], 3)
    row = buffer[0, 0:1] + buffer[1, 0:1] + buffer[2, 0:1] + buffer[3, 0:1]
    return jnp.broadcast_to(row, (ROWS, 128)).T


def kernel(
    qs, ks, vs, fs, gain, kl, ql, fl, oa, lengths,
    into, taps, out, taps_t, l_into, l_over, l_back, l_out,
    qs_adj, ks_adj, vs_adj, fs_adj, gain_adj, kl_adj, ql_adj, fl_adj,
    product, halo, after, mixed, mixed_adj, own_back, x_hat, f_hat,
    into_m, into_tm, out_m, out_tm, next_m,
    pairs_send, pairs_recv, packed_send, packed_recv, adjoint_send, adjoint_recv,
    joined_send, joined_recv, sum_send, sum_recv, all_recv, powers, inners, gains,
    spec, spec_b, held, result,
    pairs_s, pairs_r, packed_s, packed_r, adjoint_s, adjoint_r, joined_s, joined_r,
    sum_s, sum_r, all_s, all_r, halo_s, halo_r, after_s, after_r,
    power_s, power_r, inner_s, inner_r,
):
    me, col = lax.axis_index("ctx"), lax.axis_index("tp")
    barrier = pltpu.get_barrier_semaphore()

    def greet(step, carry):
        pl.semaphore_signal(
            barrier, inc=1, device_id={"ctx": (me + step) % BLOCKS}, device_id_type=MESH
        )
        return carry

    lax.fori_loop(1, BLOCKS, greet, 0)
    for step in range(1, 4):
        pl.semaphore_signal(
            barrier, inc=1, device_id={"tp": (col + step) % 4}, device_id_type=MESH
        )

    def make_product(tile, carry):
        at = lanes(tile, WIDE)
        product[:, at] = (ks[:, at].astype(F32) * vs[:, at].astype(F32)).astype(BF16)
        return carry

    lax.fori_loop(0, 2048 // WIDE, make_product, 0)
    pl.semaphore_wait(barrier, BLOCKS - 1 + 3)
    halo_copy = neighbour_copy(product, halo, (halo_s, halo_r), (me + 1) % BLOCKS)
    halo_copy.start()

    def pack_pairs(step, carry):
        tile = chip_at(me, step)
        at = lanes(tile, 128)
        up = (oa[:, at].astype(F32) * ql[:, at].astype(F32)).astype(BF16).astype(F32)
        lags = fl[:, at].astype(F32)
        side = left((ROWS, 128))
        pairs_send[2 * tile] = jnp.where(side, lags, turned(up)).astype(BF16)
        pairs_send[2 * tile + 1] = jnp.where(side, turned(lags), up).astype(BF16)
        send_block(pairs_send, pairs_recv, (pairs_s, pairs_r), me, 2 * tile)
        send_block(pairs_send, pairs_recv, (pairs_s, pairs_r), me, 2 * tile + 1)
        return carry

    lax.fori_loop(0, CHIPS, pack_pairs, 0)

    masks = mask_rows(lengths[...], me * ROWS)
    into_m[...] = masked(into[...], masks, "halo_before")
    into_tm[...] = masked(into[...], masks, "next_own").astype(F32).T.astype(BF16)
    out_m[...] = masked(out[...], masks, "halo_own")
    out_tm[...] = out_m[...].astype(F32).T.astype(BF16)
    next_m[...] = (out[0:256, :].astype(F32) * masks["next_after"]).astype(BF16)

    def short_own(tile, carry):
        at = lanes(tile, WIDE)
        x, f = product[:, at], fs[:, at]
        xs, ts = dot(into_m[256:, :], x), dot(taps[...], f)
        x_hat[256:, at] = xs.astype(BF16)
        f_hat[:, at] = ts.astype(BF16)
        re, im = complex_product((xs[:H], xs[H:]), (ts[256 : 256 + H], ts[256 + H :]))
        q = jnp.concatenate([re, im], axis=0).astype(BF16)
        mixed[:, at] = dot(out_tm[:, 256:], q) + x.astype(F32) * f[0:1, :].astype(F32)
        return carry

    lax.fori_loop(0, 2048 // WIDE, short_own, 0)
    halo_copy.wait_recv()

    def short_halo(tile, total):
        at = lanes(tile, WIDE)
        xs = dot(into_m[0:256, :], halo[:, at])
        x_hat[0:256, at] = xs.astype(BF16)
        ts = f_hat[0:256, at].astype(F32)
        re, im = complex_product((xs[:128], xs[128:]), (ts[:128], ts[128:]))
        q = jnp.concatenate([re, im], axis=0).astype(BF16)
        y = mixed[:, at] + dot(out_tm[:, 0:256], q)
        mixed[:, at] = y
        gated = qs[:, at].astype(F32) * y
        return total + jnp.sum(gated * gated, axis=1, keepdims=True)

    total = lax.fori_loop(0, 2048 // WIDE, short_halo, jnp.zeros((ROWS, 1), F32))
    send_sums(total, powers, (power_s, power_r), col)

    wait_blocks(pairs_recv, pairs_r, BLOCKS - 1)
    inner_transform(lambda j: pairs_recv[j], l_into, spec)
    scale = lax.rsqrt(take_sums(powers, (power_s, power_r)) / D + EPS)

    def pack_signal(step, carry):
        tile = chip_at(me, step)
        at = lanes(tile, 128)
        gated = qs[:, at].astype(F32) * mixed[:, at]
        s = gated * scale * gain[:, at] * kl[:, at].astype(F32)
        side = left((64, 128))
        low, high = s[:64], s[64:]
        packed_send[2 * tile] = jnp.where(side, low, turned(high)).astype(BF16)
        packed_send[2 * tile + 1] = jnp.where(side, turned(low), high).astype(BF16)
        send_block(packed_send, packed_recv, (packed_s, packed_r), me, 2 * tile)
        send_block(packed_send, packed_recv, (packed_s, packed_r), me, 2 * tile + 1)
        return carry

    lax.fori_loop(0, CHIPS, pack_signal, 0)

    def early(group, carry):
        z = outer_transform(group, l_over, spec)
        held[:, lanes(group, 128 * GROUP)] = z
        zr, zi = z[:64], z[64:]
        ur, ui = group_turned(zr), group_turned(zi)
        im = ui * zr - ur * zi
        outer_inverse(
            group, zr * ur + zi * ui, jnp.where(group_lanes(), im, -im), l_back, spec_b
        )
        return carry

    lax.fori_loop(0, 128 // GROUP, early, 0)
    inner_inverse(l_out, spec_b, result)

    def early_out(step, carry):
        tile = chip_at(me, step)
        for j in (2 * tile, 2 * tile + 1):
            later = result[jnp.minimum(j + 1, BLOCKS - 1), 128:]
            value = result[j, 0:128] - jnp.where(j < BLOCKS - 1, later, 0.0)
            adjoint_send[j] = jnp.where(left((64, 128)), value[:64], value[64:]).astype(BF16)
            send_block(adjoint_send, adjoint_recv, (adjoint_s, adjoint_r), me, j)
        return carry

    lax.fori_loop(0, CHIPS, early_out, 0)

    wait_blocks(packed_recv, packed_r, BLOCKS - 1)

    def both_halves(j):
        p = packed_recv[j].astype(F32)
        r = turned(p)
        side = left((64, 128))
        return jnp.concatenate([jnp.where(side, p, r), jnp.where(side, r, p)], axis=0).astype(BF16)

    inner_transform(both_halves, l_into, spec)

    def late(group, carry):
        s = outer_transform(group, l_over, spec)
        z = held[:, lanes(group, 128 * GROUP)]
        zr, zi = z[:64], z[64:]
        sr, si = s[:64], s[64:]
        si = jnp.where(group_lanes(), si, -si)
        outer_inverse(group, zr * sr - zi * si, zi * sr + zr * si, l_back, spec_b)
        return carry

    lax.fori_loop(0, 128 // GROUP, late, 0)
    inner_inverse(l_out, spec_b, result)

    def late_out(step, carry):
        tile = chip_at(me, step)
        for j in (2 * tile, 2 * tile + 1):
            before = jnp.where(j > 0, result[jnp.maximum(j - 1, 0), 128:], 0.0)
            later = jnp.where(j < BLOCKS - 1, result[jnp.minimum(j + 1, BLOCKS - 1), 128:], 0.0)
            value = result[j, 0:128] + jnp.where(left((ROWS, 128)), before, -later)
            joined_send[j] = value.astype(BF16)
            send_block(joined_send, joined_recv, (joined_s, joined_r), me, j)
        return carry

    lax.fori_loop(0, CHIPS, late_out, 0)

    wait_blocks(adjoint_recv, adjoint_r, BLOCKS - 1)

    def weigh(tile, total):
        at = lanes(tile, 128)
        signal_adj = unpacked(adjoint_recv, tile)
        gated = qs[:, at].astype(F32) * mixed[:, at]
        kl_adj[:, at] = (signal_adj * (gated * scale * gain[:, at])).astype(BF16)
        both = signal_adj * kl[:, at].astype(F32) * gated
        gains[:, at] = jnp.sum(both * scale, axis=0, keepdims=True)
        return total + jnp.sum(both * gain[:, at], axis=1, keepdims=True)

    total = lax.fori_loop(0, CHIPS, weigh, jnp.zeros((ROWS, 1), F32))
    send_sums(total, inners, (inner_s, inner_r), col)
    drop = scale * scale * scale * take_sums(inners, (inner_s, inner_r)) / D

    def make_mixed_adj(tile, carry):
        at = lanes(tile, 128)
        q = qs[:, at].astype(F32)
        y = mixed[:, at]
        weighted = unpacked(adjoint_recv, tile) * kl[:, at].astype(F32) * gain[:, at]
        gated_adj = scale * weighted - q * y * drop
        qs_adj[:, at] = (gated_adj * y).astype(BF16)
        mixed_adj[:, at] = (gated_adj * q).astype(BF16)
        return carry

    lax.fori_loop(0, CHIPS, make_mixed_adj, 0)
    after_copy = neighbour_copy(
        mixed_adj, after, (after_s, after_r), (me + BLOCKS - 1) % BLOCKS
    )
    after_copy.start()

    def back_own(tile, carry):
        at = lanes(tile, WIDE)
        f, m = fs[:, at], mixed_adj[:, at]
        ms = dot(out_m[...], m)
        ts = f_hat[256:, at].astype(F32)
        xs = x_hat[:, at].astype(F32)
        m_head, m_body = (ms[:128], ms[128:256]), (ms[256 : 256 + H], ms[256 + H :])
        re, im = adjoint_product(m_body, (ts[:H], ts[H:]))
        wide = m.astype(F32)
        own_back[:, at] = dot(
            into_tm[:, 256:], jnp.concatenate([re, im], axis=0).astype(BF16)
        ) + wide * f[0:1, :].astype(F32)
        g = rejoined(
            adjoint_product(m_head, (xs[:128], xs[128:256])),
            adjoint_product(m_body, (xs[256 : 256 + H], xs[256 + H :])),
        )
        zero = jnp.sum(wide * product[:, at].astype(F32), axis=0, keepdims=True)
        row = lax.broadcasted_iota(jnp.int32, (ROWS, WIDE), 0)
        part = (dot(taps_t[...], g) + jnp.where(row == 0, zero, 0.0)).astype(BF16)
        gain_rows = jnp.broadcast_to(gains[:, at], (16, WIDE)).astype(BF16)
        for i in range(WIDE // 128):
            tile_at = slice(128 * i, 128 * (i + 1))
            block = 2 * (tile * (WIDE // 128) + i)
            sum_send[block, 0:64] = part[:64, tile_at]
            sum_send[block + 1, 0:64] = part[64:, tile_at]
            sum_send[block, 64:80] = gain_rows[:, tile_at]
            sum_send[block + 1, 64:80] = gain_rows[:, tile_at]
        return carry

    lax.fori_loop(0, 2048 // WIDE, back_own, 0)

    def scatter(step, carry):
        tile = chip_at(me, step)
        send_block(sum_send, sum_recv, (sum_s, sum_r), me, 2 * tile)
        send_block(sum_send, sum_recv, (sum_s, sum_r), me, 2 * tile + 1)
        return carry

    lax.fori_loop(0, CHIPS, scatter, 0)
    after_copy.wait_recv()

    def back_halo(tile, carry):
        at = lanes(tile, WIDE)
        ms = dot(next_m[...], after[:, at])
        ts = f_hat[0:256, at].astype(F32)
        re, im = adjoint_product((ms[:128], ms[128:]), (ts[:128], ts[128:]))
        back = own_back[:, at] + dot(
            into_tm[:, 0:256], jnp.concatenate([re, im], axis=0).astype(BF16)
        )
        ks_adj[:, at] = (back * vs[:, at].astype(F32)).astype(BF16)
        vs_adj[:, at] = (back * ks[:, at].astype(F32)).astype(BF16)
        return carry

    lax.fori_loop(0, 2048 // WIDE, back_halo, 0)
    wait_blocks(sum_recv, sum_r, BLOCKS - 1)

    def add(j, total):
        return total + sum_recv[j].astype(F32)

    all_recv[me] = lax.fori_loop(0, BLOCKS, add, jnp.zeros((80, 128), F32)).astype(BF16)

    def gather(step, carry):
        tile = chip_at(me, step)
        for dest in (2 * tile, 2 * tile + 1):

            @pl.when(dest != me)
            def _():
                neighbour_copy(all_recv.at[me], all_recv.at[me], (all_s, all_r), dest).start()

        return carry

    lax.fori_loop(0, CHIPS, gather, 0)
    wait_blocks(joined_recv, joined_r, BLOCKS - 1)

    def finish(tile, carry):
        at = lanes(tile, 128)
        even, odd = joined_recv[2 * tile].astype(F32), joined_recv[2 * tile + 1].astype(F32)
        side = left((ROWS, 128))
        conv = jnp.where(side, even, turned(odd))
        ql_adj[:, at] = (oa[:, at].astype(F32) * conv).astype(BF16)
        fl_adj[:, at] = jnp.where(side, turned(even), odd).astype(BF16)
        return carry

    lax.fori_loop(0, CHIPS, finish, 0)
    wait_blocks(all_recv, all_r, BLOCKS - 1)

    def share(tile, carry):
        at = lanes(tile, 128)
        fs_adj[0:64, at] = all_recv[2 * tile, 0:64].astype(F32)
        fs_adj[64:128, at] = all_recv[2 * tile + 1, 0:64].astype(F32)
        gain_adj[:, at] = all_recv[2 * tile, 64:80].astype(F32)[0:1]
        return carry

    lax.fori_loop(0, CHIPS, share, 0)

    halo_copy.wait_send()
    after_copy.wait_send()
    wait_blocks(pairs_send, pairs_s, BLOCKS - 1)
    wait_blocks(packed_send, packed_s, BLOCKS - 1)
    wait_blocks(adjoint_send, adjoint_s, BLOCKS - 1)
    wait_blocks(joined_send, joined_s, BLOCKS - 1)
    wait_blocks(sum_send, sum_s, BLOCKS - 1)
    wait_blocks(all_recv, all_s, BLOCKS - 1)
    wait_blocks(powers, power_s, 3)
    wait_blocks(inners, inner_s, 3)


def local(qs, ks, vs, fs, gain, kl, ql, fl, oa, contig_lengths):
    tables = [jnp.asarray(table) for table in short_tables()]
    into, taps, out = tables
    operands = [
        qs, ks, vs, fs, gain[None, :], kl, ql, fl, oa, contig_lengths[None, :],
        into, taps, out, taps.T, *(jnp.asarray(table) for table in long_tables()),
    ]
    wide = ROWS, qs.shape[1]
    row = (1, wide[1])
    table, turned_table = (1152, ROWS), (ROWS, 1152)
    full, half, sums = (BLOCKS, ROWS, 128), (BLOCKS, 64, 128), (BLOCKS, 80, 128)
    spec = (BLOCKS * PITCH, 128)
    outs = [(wide, BF16)] * 3 + [(wide, F32), (row, F32)] + [(wide, BF16)] * 3
    scratch = [(wide, BF16)] * 3 + [(wide, F32), (wide, BF16), (wide, F32)]
    scratch += [((1152, wide[1]), BF16)] * 2
    scratch += [(table, BF16), (turned_table, BF16), (table, BF16), (turned_table, BF16)]
    scratch += [((256, ROWS), BF16)]
    scratch += [(full, BF16)] * 2 + [(half, BF16)] * 4 + [(full, BF16)] * 2 + [(sums, BF16)] * 3
    scratch += [((4, 8, 128), F32)] * 2 + [(row, F32)]
    scratch += [(spec, F32)] * 2 + [((128, 128 * 128), F32), ((BLOCKS, 256, 128), F32)]
    results = pl.pallas_call(
        kernel,
        out_shape=[jax.ShapeDtypeStruct(shape, dtype) for shape, dtype in outs],
        in_specs=[VMEM] * len(operands),
        out_specs=[VMEM] * len(outs),
        scratch_shapes=[pltpu.VMEM(shape, dtype) for shape, dtype in scratch]
        + [pltpu.SemaphoreType.DMA] * 20,
        compiler_params=pltpu.CompilerParams(
            collective_id=0, has_side_effects=True, vmem_limit_bytes=62 * 1024 * 1024
        ),
    )(*operands)
    qs_adj, ks_adj, vs_adj, fs_adj, gain_adj, kl_adj, ql_adj, fl_adj = results
    return qs_adj, ks_adj, vs_adj, fs_adj, gain_adj[0], kl_adj, ql_adj, fl_adj


def solution(mesh):
    spread_spec = P("ctx", "tp")
    in_specs = (
        spread_spec, spread_spec, spread_spec, P(None, "tp"), P("tp"),
        spread_spec, spread_spec, spread_spec, spread_spec, P(),
    )
    out_specs = (
        spread_spec, spread_spec, spread_spec, P(None, "tp"), P("tp"),
        spread_spec, spread_spec, spread_spec,
    )
    return jax.shard_map(local, mesh=mesh, in_specs=in_specs, out_specs=out_specs, check_vma=False)
```

```python
import math

import jax
import jax.numpy as jnp
import ml_dtypes
import numpy as np
from jax import lax
from jax.experimental import pallas as pl
from jax.experimental.pallas import tpu as pltpu
from jax.sharding import PartitionSpec as P

D = 8192
EPS = 1e-06
F32 = jnp.float32
BF16 = jnp.bfloat16
ROWS = 128
BLOCKS = 32
HALVES = (64, 32, 16, 8, 4, 2, 1)
PITCH = 264
VMEM = pl.BlockSpec(memory_space=pltpu.VMEM)


def odd_angles(size):
    return 2.0 * math.pi * (np.arange(size // 2) + 0.5) / size


def short_tables():
    into_re, into_im, taps_re, taps_im, out_re, out_im = ([] for _ in range(6))
    for half in (ROWS,) + HALVES:
        theta = odd_angles(2 * half)
        pairs = 1 if half == ROWS else ROWS // (2 * half)
        for pair in range(pairs):
            base = 0 if half == ROWS else pair * 2 * half
            first = np.zeros((half, ROWS)), np.zeros((half, ROWS))
            last = np.zeros((half, ROWS)), np.zeros((half, ROWS))
            taps = np.zeros((half, ROWS)), np.zeros((half, ROWS))
            ramp = np.arange(half)
            first[0][:, base : base + half] = np.cos(np.outer(theta, ramp))
            first[1][:, base : base + half] = -np.sin(np.outer(theta, ramp))
            start = 0 if half == ROWS else base + half
            last[0][:, start : start + half] = np.cos(np.outer(theta, ramp + half)) / half
            last[1][:, start : start + half] = -np.sin(np.outer(theta, ramp + half)) / half
            lags = np.arange(1, min(2 * half, ROWS))
            taps[0][:, lags] = np.cos(np.outer(theta, lags))
            taps[1][:, lags] = -np.sin(np.outer(theta, lags))
            for parts, pair_of in ((into_re, first), (out_re, last), (taps_re, taps)):
                parts.append(pair_of[0])
            for parts, pair_of in ((into_im, first), (out_im, last), (taps_im, taps)):
                parts.append(pair_of[1])

    def joined(re, im):
        re, im = np.concatenate(re), np.concatenate(im)
        return np.concatenate([re[:ROWS], im[:ROWS], re[ROWS:], im[ROWS:]]).astype(ml_dtypes.bfloat16)

    return joined(into_re, into_im), joined(taps_re, taps_im), joined(out_re, out_im)


def long_tables():
    theta = odd_angles(256)
    inner = np.outer(theta, np.arange(ROWS))
    into = np.concatenate([np.cos(inner), -np.sin(inner)])
    outer = np.outer(np.arange(256), theta)
    out = np.concatenate([np.cos(outer), -np.sin(outer)], axis=1) / 128.0
    angle = 2.0 * math.pi * (np.outer(np.arange(64), np.arange(BLOCKS)) % 64) / 64.0
    cos, sin = np.cos(angle), np.sin(angle)
    over = np.block([[cos, sin], [-sin, cos]])
    back = np.block([[cos.T, -sin.T], [sin.T, cos.T]]) / 64.0
    return [table.astype(ml_dtypes.bfloat16) for table in (into, over, back, out)]


def dot(a, b):
    return jnp.dot(a, b, preferred_element_type=F32)


def turned(x):
    return pltpu.roll(x, 64, 1)


def left(shape):
    return lax.broadcasted_iota(jnp.int32, shape, 1) < 64


def lanes(tile, width):
    return pl.ds(pl.multiple_of(tile * width, width), width)


def mask_rows(lengths, first):
    before = lax.broadcasted_iota(jnp.int32, (64, 64), 1) < lax.broadcasted_iota(
        jnp.int32, (64, 64), 0
    )
    starts = jnp.sum(jnp.where(before, lengths, 0), axis=1, keepdims=True)
    tokens = BLOCKS * ROWS

    def label(positions):
        place = positions + first
        begun = jnp.sum(jnp.where(place >= starts, 1, 0), axis=0, keepdims=True)
        return begun + jnp.where(place >= tokens, 1, 0)

    own = lax.broadcasted_iota(jnp.int32, (1, ROWS), 1)
    here = label(own)
    before_here = label(own - own - 1)
    last_here = label(own - own + (ROWS - 1))

    def same(a, b):
        return (a == b).astype(F32)

    halves = [same(here, label((own // (2 * half)) * (2 * half) + half - 1)) for half in HALVES]
    return dict(
        halves=halves,
        halo_own=same(here, before_here),
        halo_before=same(label(own - ROWS), before_here),
        next_own=same(here, last_here),
        next_after=same(label(own + ROWS), last_here),
    )


def spread(masks, head):
    parts = [jnp.broadcast_to(masks[head], (256, ROWS))]
    for _ in range(2):
        parts += [jnp.broadcast_to(mask, (64, ROWS)) for mask in masks["halves"]]
    return jnp.concatenate(parts, axis=0)


def masked(table, masks, head):
    return (table.astype(F32) * spread(masks, head)).astype(BF16)


H = 448


def complex_product(a, b):
    return a[0] * b[0] - a[1] * b[1], a[0] * b[1] + a[1] * b[0]


def adjoint_product(a, b):
    return a[0] * b[0] + a[1] * b[1], a[1] * b[0] - a[0] * b[1]


def split_spectrum(table, head_rows, body_rows):
    head = dot(table[0:256, :], head_rows)
    body = dot(table[256:, :], body_rows)
    return (head[:128], head[128:]), (body[:H], body[H:])


def rejoined(head, body):
    return jnp.concatenate([head[0], head[1], body[0], body[1]], axis=0).astype(BF16)


GROUP = 16
SPAN = 8
WIDE = 512
CHIPS = 16
MESH = pl.DeviceIdType.MESH


def inner_transform(read, into, spec):
    def step(j, carry):
        value = dot(into[...], jnp.concatenate([read(SPAN * j + i) for i in range(SPAN)], axis=1))
        for i in range(SPAN):
            spec[pl.ds((SPAN * j + i) * PITCH, 256), :] = value[:, 128 * i : 128 * (i + 1)]
        return carry

    lax.fori_loop(0, BLOCKS // SPAN, step, 0)


def outer_transform(group, over, spec):
    columns = []
    for member in range(GROUP):
        f = group * GROUP + member
        columns.append(
            jnp.concatenate(
                [
                    spec[pl.ds(f, BLOCKS, stride=PITCH), :],
                    spec[pl.ds(f + 128, BLOCKS, stride=PITCH), :],
                ],
                axis=0,
            )
        )
    return dot(over[...], jnp.concatenate(columns, axis=1).astype(BF16))


def outer_inverse(group, re, im, back, spec):
    result = dot(back[...], jnp.concatenate([re, im], axis=0).astype(BF16))
    for member in range(GROUP):
        f = group * GROUP + member
        piece = result[:, 128 * member : 128 * (member + 1)]
        spec[pl.ds(f, BLOCKS, stride=PITCH), :] = piece[:BLOCKS]
        spec[pl.ds(f + 128, BLOCKS, stride=PITCH), :] = piece[BLOCKS:]


def inner_inverse(out, spec, result):
    def step(j, carry):
        value = dot(
            out[...],
            jnp.concatenate(
                [spec[pl.ds((SPAN * j + i) * PITCH, 256), :].astype(BF16) for i in range(SPAN)],
                axis=1,
            ),
        )
        for i in range(SPAN):
            result[SPAN * j + i] = value[:, 128 * i : 128 * (i + 1)]
        return carry

    lax.fori_loop(0, BLOCKS // SPAN, step, 0)


def group_lanes():
    return (lax.broadcasted_iota(jnp.int32, (64, 128 * GROUP), 1) & 127) < 64


def group_turned(x):
    return jnp.concatenate(
        [turned(x[:, 128 * m : 128 * (m + 1)]) for m in range(GROUP)], axis=1
    )


def unpacked(adjoint, tile):
    even, odd = adjoint[2 * tile].astype(F32), adjoint[2 * tile + 1].astype(F32)
    side = left((64, 128))
    return jnp.concatenate(
        [jnp.where(side, even, turned(odd)), jnp.where(side, turned(even), odd)], axis=0
    )


def far_first(step):
    return jnp.where(step == 0, 2, jnp.where(step == 1, 1, jnp.where(step == 2, 3, 0)))


def chip_at(me, step):
    chip = me // 2
    return (chip // 4 + far_first(step // 4)) % 4 * 4 + (chip % 4 + far_first(step % 4)) % 4


def send_block(send, recv, sems, me, dest, own=None):
    @pl.when(dest != me)
    def _():
        pltpu.make_async_remote_copy(
            src_ref=send.at[dest],
            dst_ref=recv.at[me],
            send_sem=sems[0],
            recv_sem=sems[1],
            device_id={"ctx": dest},
            device_id_type=MESH,
        ).start()

    @pl.when(dest == me)
    def _():
        if own is None:
            recv[me] = send[me]
        else:
            pltpu.make_async_copy(send.at[me], recv.at[me], own).start()


def wait_blocks(buffer, sem, count):
    part = buffer.at[pl.ds(0, count)]
    pltpu.make_async_copy(part, part, sem).wait()


def neighbour_copy(source, target, sems, dest):
    return pltpu.make_async_remote_copy(
        src_ref=source,
        dst_ref=target,
        send_sem=sems[0],
        recv_sem=sems[1],
        device_id={"ctx": dest},
        device_id_type=MESH,
    )


def send_sums(column, buffer, sems, col):
    buffer[col] = jnp.broadcast_to(column, (ROWS, 128)).T[:8]
    for step in range(1, 4):
        pltpu.make_async_remote_copy(
            src_ref=buffer.at[col],
            dst_ref=buffer.at[col],
            send_sem=sems[0],
            recv_sem=sems[1],
            device_id={"tp": (col + step) % 4},
            device_id_type=MESH,
        ).start()


def take_sums(buffer, sems):
    wait_blocks(buffer, sems[1], 3)
    row = buffer[0, 0:1] + buffer[1, 0:1] + buffer[2, 0:1] + buffer[3, 0:1]
    return jnp.broadcast_to(row, (ROWS, 128)).T


OPERANDS = 18
STAGED = 4


def kernel(*refs):
    far = refs[:OPERANDS]
    o_joined, o_all, *o_staged = refs[OPERANDS : OPERANDS + 2 + STAGED]
    near = refs[OPERANDS + 2 + STAGED : 2 * OPERANDS + 2 + STAGED]
    (
        qs_adj, ks_adj, vs_adj, kl_adj,
        product, halo, after, mixed, mixed_adj, own_back, x_hat, f_hat,
        into_m, into_tm, out_m, out_tm, next_m,
        pairs_send, pairs_recv, packed_send, packed_recv, adjoint_send, adjoint_recv,
        joined_send, half_send, half_recv, half_own, sum_send, sum_recv, all_half,
        powers, inners, gains, spec, spec_b, held, result,
        loads, stores, half_s, half_r,
        pairs_s, pairs_r, packed_s, packed_r, adjoint_s, adjoint_r, joined_s, joined_r,
        sum_s, sum_r, all_s, all_r, halo_s, halo_r, after_s, after_r,
        power_s, power_r, inner_s, inner_r, twin_s, twin_r,
    ) = refs[2 * OPERANDS + 2 + STAGED :]
    (
        ks, vs, oa, ql, fl, lengths, fs, into, taps, out, qs, gain, kl, l_into, l_over,
        l_back, l_out, taps_t,
    ) = near

    def load(i):
        return pltpu.make_async_copy(far[i], near[i], loads.at[i])

    def store(i):
        source = (qs_adj, ks_adj, vs_adj, kl_adj)[i]
        return pltpu.make_async_copy(source, o_staged[i], stores.at[i])

    me, col = lax.axis_index("ctx"), lax.axis_index("tp")
    chip, core = me // 2, me % 2
    twin_id = 2 * chip + 1 - core
    barrier = pltpu.get_barrier_semaphore()

    def greet(step, carry):
        pl.semaphore_signal(
            barrier, inc=1, device_id={"ctx": (me + step) % BLOCKS}, device_id_type=MESH
        )
        return carry

    lax.fori_loop(1, BLOCKS, greet, 0)
    for step in range(1, 4):
        pl.semaphore_signal(
            barrier, inc=1, device_id={"tp": (col + step) % 4}, device_id_type=MESH
        )

    for i in range(OPERANDS):
        load(i).start()
    load(0).wait()
    load(1).wait()

    def make_product(tile, carry):
        at = lanes(tile, WIDE)
        product[:, at] = (ks[:, at].astype(F32) * vs[:, at].astype(F32)).astype(BF16)
        return carry

    lax.fori_loop(0, 2048 // WIDE, make_product, 0)
    pl.semaphore_wait(barrier, BLOCKS - 1 + 3)
    halo_copy = neighbour_copy(product, halo, (halo_s, halo_r), (me + 1) % BLOCKS)
    halo_copy.start()
    for i in range(2, 5):
        load(i).wait()

    def pack_pairs(step, carry):
        tile = chip_at(me, step)
        at = lanes(tile, 128)
        up = (oa[:, at].astype(F32) * ql[:, at].astype(F32)).astype(BF16).astype(F32)
        lags = fl[:, at].astype(F32)
        side = left((ROWS, 128))
        pairs_send[2 * tile] = jnp.where(side, lags, turned(up)).astype(BF16)
        pairs_send[2 * tile + 1] = jnp.where(side, turned(lags), up).astype(BF16)
        send_block(pairs_send, pairs_recv, (pairs_s, pairs_r), me, 2 * tile)
        send_block(pairs_send, pairs_recv, (pairs_s, pairs_r), me, 2 * tile + 1)
        return carry

    lax.fori_loop(0, CHIPS, pack_pairs, 0)

    for i in range(5, OPERANDS):
        load(i).wait()
    masks = mask_rows(lengths[...], me * ROWS)
    into_m[...] = masked(into[...], masks, "halo_before")
    into_tm[...] = masked(into[...], masks, "next_own").astype(F32).T.astype(BF16)
    out_m[...] = masked(out[...], masks, "halo_own")
    out_tm[...] = out_m[...].astype(F32).T.astype(BF16)
    next_m[...] = (out[0:256, :].astype(F32) * masks["next_after"]).astype(BF16)

    def short_own(tile, carry):
        at = lanes(tile, WIDE)
        x, f = product[:, at], fs[:, at]
        xs, ts = dot(into_m[256:, :], x), dot(taps[...], f)
        x_hat[256:, at] = xs.astype(BF16)
        f_hat[:, at] = ts.astype(BF16)
        re, im = complex_product((xs[:H], xs[H:]), (ts[256 : 256 + H], ts[256 + H :]))
        q = jnp.concatenate([re, im], axis=0).astype(BF16)
        mixed[:, at] = dot(out_tm[:, 256:], q) + x.astype(F32) * f[0:1, :].astype(F32)
        return carry

    lax.fori_loop(0, 2048 // WIDE, short_own, 0)
    halo_copy.wait_recv()

    def short_halo(tile, total):
        at = lanes(tile, WIDE)
        xs = dot(into_m[0:256, :], halo[:, at])
        x_hat[0:256, at] = xs.astype(BF16)
        ts = f_hat[0:256, at].astype(F32)
        re, im = complex_product((xs[:128], xs[128:]), (ts[:128], ts[128:]))
        q = jnp.concatenate([re, im], axis=0).astype(BF16)
        y = mixed[:, at] + dot(out_tm[:, 0:256], q)
        mixed[:, at] = y
        gated = qs[:, at].astype(F32) * y
        return total + jnp.sum(gated * gated, axis=1, keepdims=True)

    total = lax.fori_loop(0, 2048 // WIDE, short_halo, jnp.zeros((ROWS, 1), F32))
    send_sums(total, powers, (power_s, power_r), col)

    scale = lax.rsqrt(take_sums(powers, (power_s, power_r)) / D + EPS)

    def pack_signal(step, carry):
        tile = chip_at(me, step)
        at = lanes(tile, 128)
        gated = qs[:, at].astype(F32) * mixed[:, at]
        s = gated * scale * gain[:, at] * kl[:, at].astype(F32)
        side = left((64, 128))
        low, high = s[:64], s[64:]
        packed_send[2 * tile] = jnp.where(side, low, turned(high)).astype(BF16)
        packed_send[2 * tile + 1] = jnp.where(side, turned(low), high).astype(BF16)
        send_block(packed_send, packed_recv, (packed_s, packed_r), me, 2 * tile)
        send_block(packed_send, packed_recv, (packed_s, packed_r), me, 2 * tile + 1)
        return carry

    lax.fori_loop(0, CHIPS, pack_signal, 0)
    wait_blocks(pairs_recv, pairs_r, BLOCKS - 1)
    inner_transform(lambda j: pairs_recv[j], l_into, spec)

    def early(group, carry):
        z = outer_transform(group, l_over, spec)
        held[:, lanes(group, 128 * GROUP)] = z
        zr, zi = z[:64], z[64:]
        ur, ui = group_turned(zr), group_turned(zi)
        im = ui * zr - ur * zi
        outer_inverse(
            group, zr * ur + zi * ui, jnp.where(group_lanes(), im, -im), l_back, spec_b
        )
        return carry

    lax.fori_loop(0, 128 // GROUP, early, 0)
    inner_inverse(l_out, spec_b, result)

    def early_out(step, carry):
        tile = chip_at(me, step)
        for j in (2 * tile, 2 * tile + 1):
            later = result[jnp.minimum(j + 1, BLOCKS - 1), 128:]
            value = result[j, 0:128] - jnp.where(j < BLOCKS - 1, later, 0.0)
            adjoint_send[j] = jnp.where(left((64, 128)), value[:64], value[64:]).astype(BF16)
            send_block(adjoint_send, adjoint_recv, (adjoint_s, adjoint_r), me, j)
        return carry

    lax.fori_loop(0, CHIPS, early_out, 0)

    wait_blocks(packed_recv, packed_r, BLOCKS - 1)

    def both_halves(j):
        p = packed_recv[j].astype(F32)
        r = turned(p)
        side = left((64, 128))
        return jnp.concatenate([jnp.where(side, p, r), jnp.where(side, r, p)], axis=0).astype(BF16)

    inner_transform(both_halves, l_into, spec)

    def late(group, carry):
        s = outer_transform(group, l_over, spec)
        z = held[:, lanes(group, 128 * GROUP)]
        zr, zi = z[:64], z[64:]
        sr, si = s[:64], s[64:]
        si = jnp.where(group_lanes(), si, -si)
        outer_inverse(group, zr * sr - zi * si, zi * sr + zr * si, l_back, spec_b)
        return carry

    lax.fori_loop(0, 128 // GROUP, late, 0)
    inner_inverse(l_out, spec_b, result)

    def late_out(step, carry):
        tile = chip_at(me, step)
        for j in (2 * tile, 2 * tile + 1):
            before = jnp.where(j > 0, result[jnp.maximum(j - 1, 0), 128:], 0.0)
            later = jnp.where(j < BLOCKS - 1, result[jnp.minimum(j + 1, BLOCKS - 1), 128:], 0.0)
            value = result[j, 0:128] + jnp.where(left((ROWS, 128)), before, -later)
            joined_send[j] = value.astype(BF16)
            send_block(
                joined_send, o_joined, (joined_s, joined_r), me, j, stores.at[STAGED]
            )
        return carry

    lax.fori_loop(0, CHIPS, late_out, 0)

    wait_blocks(adjoint_recv, adjoint_r, BLOCKS - 1)

    def weigh(tile, total):
        at = lanes(tile, 128)
        signal_adj = unpacked(adjoint_recv, tile)
        gated = qs[:, at].astype(F32) * mixed[:, at]
        kl_adj[:, at] = (signal_adj * (gated * scale * gain[:, at])).astype(BF16)
        both = signal_adj * kl[:, at].astype(F32) * gated
        gains[:, at] = jnp.sum(both * scale, axis=0, keepdims=True)
        return total + jnp.sum(both * gain[:, at], axis=1, keepdims=True)

    total = lax.fori_loop(0, CHIPS, weigh, jnp.zeros((ROWS, 1), F32))
    send_sums(total, inners, (inner_s, inner_r), col)
    drop = scale * scale * scale * take_sums(inners, (inner_s, inner_r)) / D

    def make_mixed_adj(tile, carry):
        at = lanes(tile, 128)
        q = qs[:, at].astype(F32)
        y = mixed[:, at]
        weighted = unpacked(adjoint_recv, tile) * kl[:, at].astype(F32) * gain[:, at]
        gated_adj = scale * weighted - q * y * drop
        qs_adj[:, at] = (gated_adj * y).astype(BF16)
        mixed_adj[:, at] = (gated_adj * q).astype(BF16)
        return carry

    lax.fori_loop(0, CHIPS, make_mixed_adj, 0)
    after_copy = neighbour_copy(
        mixed_adj, after, (after_s, after_r), (me + BLOCKS - 1) % BLOCKS
    )
    after_copy.start()
    store(0).start()
    store(3).start()

    def half_copy(tile):
        part = pl.ds(tile * (WIDE // 128), WIDE // 128)
        return neighbour_copy(
            half_send.at[part], half_recv.at[part], (half_s.at[tile], half_r.at[tile]), twin_id
        )

    def back_own(tile, carry):
        at = lanes(tile, WIDE)
        f, m = fs[:, at], mixed_adj[:, at]
        ms = dot(out_m[...], m)
        ts = f_hat[256:, at].astype(F32)
        xs = x_hat[:, at].astype(F32)
        m_head, m_body = (ms[:128], ms[128:256]), (ms[256 : 256 + H], ms[256 + H :])
        re, im = adjoint_product(m_body, (ts[:H], ts[H:]))
        wide = m.astype(F32)
        own_back[:, at] = dot(
            into_tm[:, 256:], jnp.concatenate([re, im], axis=0).astype(BF16)
        ) + wide * f[0:1, :].astype(F32)
        g = rejoined(
            adjoint_product(m_head, (xs[:128], xs[128:256])),
            adjoint_product(m_body, (xs[256 : 256 + H], xs[256 + H :])),
        )
        zero = jnp.sum(wide * product[:, at].astype(F32), axis=0, keepdims=True)
        row = lax.broadcasted_iota(jnp.int32, (ROWS, WIDE), 0)
        part = dot(taps_t[...], g) + jnp.where(row == 0, zero, 0.0)
        gain_rows = jnp.broadcast_to(gains[:, at], (16, WIDE))
        mine = jnp.concatenate([jnp.where(core == 0, part[:64], part[64:]), gain_rows], axis=0)
        twin = jnp.concatenate([jnp.where(core == 0, part[64:], part[:64]), gain_rows], axis=0)
        for i in range(WIDE // 128):
            tile_at = slice(128 * i, 128 * (i + 1))
            half_own[tile * (WIDE // 128) + i] = mine[:, tile_at]
            half_send[tile * (WIDE // 128) + i] = twin[:, tile_at].astype(BF16)
        half_copy(tile).start()
        return carry

    lax.fori_loop(0, 2048 // WIDE, back_own, 0)
    for tile in range(2048 // WIDE):
        half_copy(tile).wait_recv()

    def scatter(step, carry):
        dest = chip_at(me, step)
        sum_send[dest] = (half_own[dest] + half_recv[dest].astype(F32)).astype(BF16)

        @pl.when(dest != chip)
        def _():
            neighbour_copy(
                sum_send.at[dest], sum_recv.at[chip], (sum_s, sum_r), 2 * dest + core
            ).start()

        @pl.when(dest == chip)
        def _():
            sum_recv[chip] = sum_send[chip]

        return carry

    lax.fori_loop(0, CHIPS, scatter, 0)
    after_copy.wait_recv()

    def back_halo(tile, carry):
        at = lanes(tile, WIDE)
        ms = dot(next_m[...], after[:, at])
        ts = f_hat[0:256, at].astype(F32)
        re, im = adjoint_product((ms[:128], ms[128:]), (ts[:128], ts[128:]))
        back = own_back[:, at] + dot(
            into_tm[:, 0:256], jnp.concatenate([re, im], axis=0).astype(BF16)
        )
        ks_adj[:, at] = (back * vs[:, at].astype(F32)).astype(BF16)
        vs_adj[:, at] = (back * ks[:, at].astype(F32)).astype(BF16)
        return carry

    lax.fori_loop(0, 2048 // WIDE, back_halo, 0)
    store(1).start()
    store(2).start()
    wait_blocks(sum_recv, sum_r, CHIPS - 1)

    def add(j, total):
        return total + sum_recv[j].astype(F32)

    all_half[core, chip] = lax.fori_loop(0, CHIPS, add, jnp.zeros((80, 128), F32)).astype(BF16)

    def gather(step, carry):
        dest = chip_at(me, step)

        @pl.when(dest != chip)
        def _():
            block = all_half.at[core, chip]
            neighbour_copy(block, block, (all_s, all_r), 2 * dest + core).start()

        return carry

    lax.fori_loop(0, CHIPS, gather, 0)
    wait_blocks(all_half.at[core], all_r, CHIPS - 1)
    twin_copy = neighbour_copy(
        all_half.at[core], all_half.at[core], (twin_s, twin_r), twin_id
    )
    twin_copy.start()
    half_out = pltpu.make_async_copy(all_half.at[core], o_all.at[core], loads.at[0])
    half_out.start()
    twin_copy.wait_recv()
    other_out = pltpu.make_async_copy(
        all_half.at[1 - core], o_all.at[1 - core], loads.at[1]
    )
    other_out.start()
    wait_blocks(o_joined, joined_r, BLOCKS - 1)
    pltpu.make_async_copy(joined_send.at[me], o_joined.at[me], stores.at[STAGED]).wait()
    for i in range(STAGED):
        store(i).wait()
    half_out.wait()
    other_out.wait()
    twin_copy.wait_send()
    for tile in range(2048 // WIDE):
        half_copy(tile).wait_send()
    halo_copy.wait_send()
    after_copy.wait_send()
    wait_blocks(pairs_send, pairs_s, BLOCKS - 1)
    wait_blocks(packed_send, packed_s, BLOCKS - 1)
    wait_blocks(adjoint_send, adjoint_s, BLOCKS - 1)
    wait_blocks(joined_send, joined_s, BLOCKS - 1)
    wait_blocks(sum_send, sum_s, CHIPS - 1)
    wait_blocks(all_half.at[core], all_s, CHIPS - 1)
    wait_blocks(powers, power_s, 3)
    wait_blocks(inners, inner_s, 3)


def finish_kernel(
    joined, sums, oa, qs_in, ks_in, vs_in, kl_in,
    qs_adj, ks_adj, vs_adj, fs_adj, gain_adj, kl_adj, ql_adj, fl_adj,
):
    qs_adj[...] = qs_in[...]
    ks_adj[...] = ks_in[...]
    vs_adj[...] = vs_in[...]
    kl_adj[...] = kl_in[...]
    side = left((ROWS, 128))
    for tile in range(WIDE // 128):
        at = slice(128 * tile, 128 * (tile + 1))
        even, odd = joined[2 * tile].astype(F32), joined[2 * tile + 1].astype(F32)
        conv = jnp.where(side, even, turned(odd))
        ql_adj[:, at] = (oa[:, at].astype(F32) * conv).astype(BF16)
        fl_adj[:, at] = jnp.where(side, turned(even), odd).astype(BF16)
        fs_adj[0:64, at] = sums[0, tile, 0:64].astype(F32)
        fs_adj[64:128, at] = sums[1, tile, 0:64].astype(F32)
        gain_adj[:, at] = sums[0, tile, 64:80].astype(F32)[0:1]


def local(qs, ks, vs, fs, gain, kl, ql, fl, oa, contig_lengths):
    into, taps, out = (jnp.asarray(table) for table in short_tables())
    operands = [
        ks, vs, oa, ql, fl, contig_lengths[None, :], fs, into, taps, out, qs, gain[None, :], kl,
        *(jnp.asarray(table) for table in long_tables()), taps.T,
    ]
    wide = ROWS, qs.shape[1]
    row = (1, wide[1])
    table, turned_table = (1152, ROWS), (ROWS, 1152)
    full, half, sums = (BLOCKS, ROWS, 128), (BLOCKS, 64, 128), (CHIPS, 80, 128)
    spec = (BLOCKS * PITCH, 128)
    outs = [(full, BF16), ((2,) + sums, BF16)] + [(wide, BF16)] * STAGED
    scratch = [(operand.shape, operand.dtype) for operand in operands]
    scratch += [(wide, BF16)] * STAGED
    scratch += [(wide, BF16)] * 3 + [(wide, F32), (wide, BF16), (wide, F32)]
    scratch += [((1152, wide[1]), BF16)] * 2
    scratch += [(table, BF16), (turned_table, BF16), (table, BF16), (turned_table, BF16)]
    scratch += [((256, ROWS), BF16)]
    scratch += [(full, BF16)] * 2 + [(half, BF16)] * 4 + [(full, BF16)]
    scratch += [(sums, BF16)] * 2 + [(sums, F32)] + [(sums, BF16)] * 2 + [((2,) + sums, BF16)]
    scratch += [((4, 8, 128), F32)] * 2 + [(row, F32)]
    scratch += [(spec, F32)] * 2 + [((128, 128 * 128), F32), ((BLOCKS, 256, 128), F32)]
    anywhere = pl.BlockSpec(memory_space=pl.ANY)
    dma = pltpu.SemaphoreType.DMA
    joined, shared, *staged = pl.pallas_call(
        kernel,
        out_shape=[jax.ShapeDtypeStruct(shape, dtype) for shape, dtype in outs],
        in_specs=[anywhere] * OPERANDS,
        out_specs=[anywhere] * len(outs),
        scratch_shapes=[pltpu.VMEM(shape, dtype) for shape, dtype in scratch]
        + [dma((OPERANDS,)), dma((STAGED + 1,)), dma((4,)), dma((4,))]
        + [dma] * 22,
        compiler_params=pltpu.CompilerParams(
            collective_id=0, has_side_effects=True, vmem_limit_bytes=62 * 1024 * 1024
        ),
    )(*operands)
    tiles = WIDE // 128
    plain = pl.BlockSpec((ROWS, WIDE), lambda i: (0, i))
    line = pl.BlockSpec((1, WIDE), lambda i: (0, i))
    results = pl.pallas_call(
        finish_kernel,
        grid=(wide[1] // WIDE,),
        out_shape=[jax.ShapeDtypeStruct(wide, BF16)] * 3
        + [jax.ShapeDtypeStruct(wide, F32), jax.ShapeDtypeStruct(row, F32)]
        + [jax.ShapeDtypeStruct(wide, BF16)] * 3,
        in_specs=[
            pl.BlockSpec((2 * tiles, ROWS, 128), lambda i: (i, 0, 0)),
            pl.BlockSpec((2, tiles, 80, 128), lambda i: (0, i, 0, 0)),
        ]
        + [plain] * 5,
        out_specs=[plain] * 4 + [line] + [plain] * 3,
    )(joined, shared, oa, *staged)
    qs_adj, ks_adj, vs_adj, fs_adj, gain_adj, kl_adj, ql_adj, fl_adj = results
    return qs_adj, ks_adj, vs_adj, fs_adj, gain_adj[0], kl_adj, ql_adj, fl_adj


def solution(mesh):
    spread_spec = P("ctx", "tp")
    in_specs = (
        spread_spec, spread_spec, spread_spec, P(None, "tp"), P("tp"),
        spread_spec, spread_spec, spread_spec, spread_spec, P(),
    )
    out_specs = (
        spread_spec, spread_spec, spread_spec, P(None, "tp"), P("tp"),
        spread_spec, spread_spec, spread_spec,
    )
    return jax.shard_map(local, mesh=mesh, in_specs=in_specs, out_specs=out_specs, check_vma=False)
```

```python
import math

import jax
import jax.numpy as jnp
import ml_dtypes
import numpy as np
from jax import lax
from jax.experimental import pallas as pl
from jax.experimental.pallas import tpu as pltpu
from jax.sharding import PartitionSpec as P

D = 8192
EPS = 1e-06
F32 = jnp.float32
BF16 = jnp.bfloat16
ROWS = 128
BLOCKS = 32
HALVES = (64, 32, 16, 8, 4, 2, 1)
PITCH = 264
VMEM = pl.BlockSpec(memory_space=pltpu.VMEM)


def odd_angles(size):
    return 2.0 * math.pi * (np.arange(size // 2) + 0.5) / size


def short_tables():
    into_re, into_im, taps_re, taps_im, out_re, out_im = ([] for _ in range(6))
    for half in (ROWS,) + HALVES:
        theta = odd_angles(2 * half)
        pairs = 1 if half == ROWS else ROWS // (2 * half)
        for pair in range(pairs):
            base = 0 if half == ROWS else pair * 2 * half
            first = np.zeros((half, ROWS)), np.zeros((half, ROWS))
            last = np.zeros((half, ROWS)), np.zeros((half, ROWS))
            taps = np.zeros((half, ROWS)), np.zeros((half, ROWS))
            ramp = np.arange(half)
            first[0][:, base : base + half] = np.cos(np.outer(theta, ramp))
            first[1][:, base : base + half] = -np.sin(np.outer(theta, ramp))
            start = 0 if half == ROWS else base + half
            last[0][:, start : start + half] = np.cos(np.outer(theta, ramp + half)) / half
            last[1][:, start : start + half] = -np.sin(np.outer(theta, ramp + half)) / half
            lags = np.arange(1, min(2 * half, ROWS))
            taps[0][:, lags] = np.cos(np.outer(theta, lags))
            taps[1][:, lags] = -np.sin(np.outer(theta, lags))
            for parts, pair_of in ((into_re, first), (out_re, last), (taps_re, taps)):
                parts.append(pair_of[0])
            for parts, pair_of in ((into_im, first), (out_im, last), (taps_im, taps)):
                parts.append(pair_of[1])

    def joined(re, im):
        re, im = np.concatenate(re), np.concatenate(im)
        return np.concatenate([re[:ROWS], im[:ROWS], re[ROWS:], im[ROWS:]]).astype(ml_dtypes.bfloat16)

    return joined(into_re, into_im), joined(taps_re, taps_im), joined(out_re, out_im)


def long_tables():
    theta = odd_angles(256)
    inner = np.outer(theta, np.arange(ROWS))
    into = np.concatenate([np.cos(inner), -np.sin(inner)])
    outer = np.outer(np.arange(256), theta)
    out = np.concatenate([np.cos(outer), -np.sin(outer)], axis=1) / 128.0
    angle = 2.0 * math.pi * (np.outer(np.arange(64), np.arange(BLOCKS)) % 64) / 64.0
    cos, sin = np.cos(angle), np.sin(angle)
    over = np.block([[cos, sin], [-sin, cos]])
    back = np.block([[cos.T, -sin.T], [sin.T, cos.T]]) / 64.0
    return [table.astype(ml_dtypes.bfloat16) for table in (into, over, back, out)]


def dot(a, b):
    return jnp.dot(a, b, preferred_element_type=F32)


def turned(x):
    return pltpu.roll(x, 64, 1)


def left(shape):
    return lax.broadcasted_iota(jnp.int32, shape, 1) < 64


def lanes(tile, width):
    return pl.ds(pl.multiple_of(tile * width, width), width)


def mask_rows(lengths, first):
    before = lax.broadcasted_iota(jnp.int32, (64, 64), 1) < lax.broadcasted_iota(
        jnp.int32, (64, 64), 0
    )
    starts = jnp.sum(jnp.where(before, lengths, 0), axis=1, keepdims=True)
    tokens = BLOCKS * ROWS

    def label(positions):
        place = positions + first
        begun = jnp.sum(jnp.where(place >= starts, 1, 0), axis=0, keepdims=True)
        return begun + jnp.where(place >= tokens, 1, 0)

    own = lax.broadcasted_iota(jnp.int32, (1, ROWS), 1)
    here = label(own)
    before_here = label(own - own - 1)
    last_here = label(own - own + (ROWS - 1))

    def same(a, b):
        return (a == b).astype(F32)

    halves = [same(here, label((own // (2 * half)) * (2 * half) + half - 1)) for half in HALVES]
    return dict(
        halves=halves,
        halo_own=same(here, before_here),
        halo_before=same(label(own - ROWS), before_here),
        next_own=same(here, last_here),
        next_after=same(label(own + ROWS), last_here),
    )


def spread(masks, head):
    parts = [jnp.broadcast_to(masks[head], (256, ROWS))]
    for _ in range(2):
        parts += [jnp.broadcast_to(mask, (64, ROWS)) for mask in masks["halves"]]
    return jnp.concatenate(parts, axis=0)


def masked(table, masks, head):
    return (table.astype(F32) * spread(masks, head)).astype(BF16)


H = 448


def complex_product(a, b):
    return a[0] * b[0] - a[1] * b[1], a[0] * b[1] + a[1] * b[0]


def adjoint_product(a, b):
    return a[0] * b[0] + a[1] * b[1], a[1] * b[0] - a[0] * b[1]


def split_spectrum(table, head_rows, body_rows):
    head = dot(table[0:256, :], head_rows)
    body = dot(table[256:, :], body_rows)
    return (head[:128], head[128:]), (body[:H], body[H:])


def rejoined(head, body):
    return jnp.concatenate([head[0], head[1], body[0], body[1]], axis=0).astype(BF16)


GROUP = 16
SPAN = 8
WIDE = 512
BIG = 1024
CHIPS = 16
MESH = pl.DeviceIdType.MESH


def inner_transform(read, into, spec):
    def step(j, carry):
        value = dot(into[...], jnp.concatenate([read(SPAN * j + i) for i in range(SPAN)], axis=1))
        for i in range(SPAN):
            spec[pl.ds((SPAN * j + i) * PITCH, 256), :] = value[:, 128 * i : 128 * (i + 1)]
        return carry

    lax.fori_loop(0, BLOCKS // SPAN, step, 0)


def outer_transform(group, over, spec):
    columns = []
    for member in range(GROUP):
        f = group * GROUP + member
        columns.append(
            jnp.concatenate(
                [
                    spec[pl.ds(f, BLOCKS, stride=PITCH), :],
                    spec[pl.ds(f + 128, BLOCKS, stride=PITCH), :],
                ],
                axis=0,
            )
        )
    return dot(over[...], jnp.concatenate(columns, axis=1).astype(BF16))


def outer_inverse(group, re, im, back, spec):
    result = dot(back[...], jnp.concatenate([re, im], axis=0).astype(BF16))
    for member in range(GROUP):
        f = group * GROUP + member
        piece = result[:, 128 * member : 128 * (member + 1)]
        spec[pl.ds(f, BLOCKS, stride=PITCH), :] = piece[:BLOCKS]
        spec[pl.ds(f + 128, BLOCKS, stride=PITCH), :] = piece[BLOCKS:]


def inner_inverse(out, spec, result):
    def step(j, carry):
        value = dot(
            out[...],
            jnp.concatenate(
                [spec[pl.ds((SPAN * j + i) * PITCH, 256), :].astype(BF16) for i in range(SPAN)],
                axis=1,
            ),
        )
        for i in range(SPAN):
            result[SPAN * j + i] = value[:, 128 * i : 128 * (i + 1)]
        return carry

    lax.fori_loop(0, BLOCKS // SPAN, step, 0)


def group_lanes():
    return (lax.broadcasted_iota(jnp.int32, (64, 128 * GROUP), 1) & 127) < 64


def group_turned(x):
    return jnp.concatenate(
        [turned(x[:, 128 * m : 128 * (m + 1)]) for m in range(GROUP)], axis=1
    )


def unpacked(adjoint, tile):
    even, odd = adjoint[2 * tile].astype(F32), adjoint[2 * tile + 1].astype(F32)
    side = left((64, 128))
    return jnp.concatenate(
        [jnp.where(side, even, turned(odd)), jnp.where(side, turned(even), odd)], axis=0
    )


def far_first(step):
    return jnp.where(step == 0, 2, jnp.where(step == 1, 1, jnp.where(step == 2, 3, 0)))


def chip_at(me, step):
    chip = me // 2
    return (chip // 4 + far_first(step // 4)) % 4 * 4 + (chip % 4 + far_first(step % 4)) % 4


def send_block(send, recv, sems, me, dest):
    @pl.when(dest != me)
    def _():
        pltpu.make_async_remote_copy(
            src_ref=send.at[dest],
            dst_ref=recv.at[me],
            send_sem=sems[0],
            recv_sem=sems[1],
            device_id={"ctx": dest},
            device_id_type=MESH,
        ).start()

    @pl.when(dest == me)
    def _():
        recv[me] = send[me]


def wait_blocks(buffer, sem, count):
    part = buffer.at[pl.ds(0, count)]
    pltpu.make_async_copy(part, part, sem).wait()


def neighbour_copy(source, target, sems, dest):
    return pltpu.make_async_remote_copy(
        src_ref=source,
        dst_ref=target,
        send_sem=sems[0],
        recv_sem=sems[1],
        device_id={"ctx": dest},
        device_id_type=MESH,
    )


def send_sums(column, buffer, sems, col):
    buffer[col] = jnp.broadcast_to(column, (ROWS, 128)).T[:8]
    for step in range(1, 4):
        pltpu.make_async_remote_copy(
            src_ref=buffer.at[col],
            dst_ref=buffer.at[col],
            send_sem=sems[0],
            recv_sem=sems[1],
            device_id={"tp": (col + step) % 4},
            device_id_type=MESH,
        ).start()


def take_sums(buffer, sems):
    wait_blocks(buffer, sems[1], 3)
    row = buffer[0, 0:1] + buffer[1, 0:1] + buffer[2, 0:1] + buffer[3, 0:1]
    return jnp.broadcast_to(row, (ROWS, 128)).T


OPERANDS = 18
STAGED = 6
BATCH = 4


def kernel(*refs):
    far = refs[:OPERANDS]
    o_all, *o_staged = refs[OPERANDS : OPERANDS + 1 + STAGED]
    near = refs[OPERANDS + 1 + STAGED : 2 * OPERANDS + 1 + STAGED]
    (
        qs_adj, ks_adj, vs_adj, kl_adj, ql_adj, fl_adj,
        product, halo, after, mixed, mixed_adj, x_hat, f_hat,
        into_m, into_tm, out_m, out_tm, next_m,
        pairs_send, pairs_recv, packed_send, packed_recv, adjoint_send, adjoint_recv,
        joined_send, joined_recv, half_send, half_recv, half_own, sum_send, sum_recv, all_half,
        powers, inners, gains, spec, spec_b, held, result,
        loads, stores, half_s, half_r, halo_s, halo_r, after_s, after_r, all_r,
        pairs_s, pairs_r, packed_s, packed_r, adjoint_s, adjoint_r, joined_s, joined_r,
        sum_s, sum_r, all_s,
        power_s, power_r, inner_s, inner_r, twin_s, twin_r,
    ) = refs[2 * OPERANDS + 1 + STAGED :]
    (
        ks, vs, oa, ql, fl, lengths, fs, into, taps, out, qs, gain, kl, l_into, l_over,
        l_back, l_out, taps_t,
    ) = near

    def load(i):
        return pltpu.make_async_copy(far[i], near[i], loads.at[i])

    def store(i):
        source = (qs_adj, ks_adj, vs_adj, kl_adj, ql_adj, fl_adj)[i]
        return pltpu.make_async_copy(source, o_staged[i], stores.at[i])

    me, col = lax.axis_index("ctx"), lax.axis_index("tp")
    chip, core = me // 2, me % 2
    twin_id = 2 * chip + 1 - core
    barrier = pltpu.get_barrier_semaphore()
    for i in range(OPERANDS):
        load(i).start()

    def greet(step, carry):
        pl.semaphore_signal(
            barrier, inc=1, device_id={"ctx": (me + step) % BLOCKS}, device_id_type=MESH
        )
        return carry

    lax.fori_loop(1, BLOCKS, greet, 0)
    for step in range(1, 4):
        pl.semaphore_signal(
            barrier, inc=1, device_id={"tp": (col + step) % 4}, device_id_type=MESH
        )

    load(0).wait()
    load(1).wait()

    def make_product(tile, carry):
        at = lanes(tile, WIDE)
        product[:, at] = (ks[:, at].astype(F32) * vs[:, at].astype(F32)).astype(BF16)
        return carry

    lax.fori_loop(0, 2048 // WIDE, make_product, 0)
    pl.semaphore_wait(barrier, BLOCKS - 1 + 3)

    def halo_copy(tile):
        part = product.at[:, lanes(tile, WIDE)], halo.at[:, lanes(tile, WIDE)]
        return neighbour_copy(*part, (halo_s.at[tile], halo_r.at[tile]), (me + 1) % BLOCKS)

    def after_copy(tile):
        part = mixed_adj.at[:, lanes(tile, WIDE)], after.at[:, lanes(tile, WIDE)]
        dest = (me + BLOCKS - 1) % BLOCKS
        return neighbour_copy(*part, (after_s.at[tile], after_r.at[tile]), dest)

    for tile in range(2048 // WIDE):
        halo_copy(tile).start()
    for i in range(2, 5):
        load(i).wait()

    def pack_pairs(batch, carry):
        deep = (chip % 4 + 4 - batch) % 4
        tiles = [(chip // 4 + i) % 4 * 4 + deep for i in (2, 1, 3, 0)]
        side = left((ROWS, 128))
        for tile in tiles:
            at = lanes(tile, 128)
            up = (oa[:, at].astype(F32) * ql[:, at].astype(F32)).astype(BF16).astype(F32)
            lags = fl[:, at].astype(F32)
            pairs_send[2 * tile] = jnp.where(side, lags, turned(up)).astype(BF16)
            pairs_send[2 * tile + 1] = jnp.where(side, turned(lags), up).astype(BF16)
        for tile in tiles:
            send_block(pairs_send, pairs_recv, (pairs_s, pairs_r), me, 2 * tile)
            send_block(pairs_send, pairs_recv, (pairs_s, pairs_r), me, 2 * tile + 1)
        return carry

    lax.fori_loop(0, 1, pack_pairs, 0)

    for i in range(5, OPERANDS):
        load(i).wait()
    masks = mask_rows(lengths[...], me * ROWS)
    into_m[...] = masked(into[...], masks, "halo_before")
    into_tm[...] = masked(into[...], masks, "next_own").astype(F32).T.astype(BF16)
    out_m[...] = masked(out[...], masks, "halo_own")
    out_tm[...] = out_m[...].astype(F32).T.astype(BF16)
    next_m[...] = (out[0:256, :].astype(F32) * masks["next_after"]).astype(BF16)

    def short_own(tile, carry):
        at = lanes(tile, WIDE)
        x, f = product[:, at], fs[:, at]
        xs, ts = dot(into_m[256:, :], x), dot(taps[...], f)
        x_hat[256:, at] = xs.astype(BF16)
        f_hat[:, at] = ts.astype(BF16)
        re, im = complex_product((xs[:H], xs[H:]), (ts[256 : 256 + H], ts[256 + H :]))
        q = jnp.concatenate([re, im], axis=0).astype(BF16)
        mixed[:, at] = dot(out_tm[:, 256:], q) + x.astype(F32) * f[0:1, :].astype(F32)
        return carry

    lax.fori_loop(0, 2048 // WIDE, short_own, 0)
    for tile in range(2048 // WIDE):
        halo_copy(tile).wait_recv()
    lax.fori_loop(1, CHIPS // BATCH, pack_pairs, 0)

    def short_halo(tile, total):
        at = lanes(tile, WIDE)
        xs = dot(into_m[0:256, :], halo[:, at])
        x_hat[0:256, at] = xs.astype(BF16)
        ts = f_hat[0:256, at].astype(F32)
        re, im = complex_product((xs[:128], xs[128:]), (ts[:128], ts[128:]))
        q = jnp.concatenate([re, im], axis=0).astype(BF16)
        y = mixed[:, at] + dot(out_tm[:, 0:256], q)
        mixed[:, at] = y
        gated = qs[:, at].astype(F32) * y
        return total + jnp.sum(gated * gated, axis=1, keepdims=True)

    total = lax.fori_loop(0, 2048 // WIDE, short_halo, jnp.zeros((ROWS, 1), F32))
    send_sums(total, powers, (power_s, power_r), col)

    scale = lax.rsqrt(take_sums(powers, (power_s, power_r)) / D + EPS)

    def pack_signal(batch, carry):
        tiles = [batch * BATCH + i for i in range(BATCH)]
        side = left((64, 128))
        for tile in tiles:
            at = lanes(tile, 128)
            gated = qs[:, at].astype(F32) * mixed[:, at]
            s = gated * scale * gain[:, at] * kl[:, at].astype(F32)
            low, high = s[:64], s[64:]
            packed_send[2 * tile] = jnp.where(side, low, turned(high)).astype(BF16)
            packed_send[2 * tile + 1] = jnp.where(side, turned(low), high).astype(BF16)
        return carry

    lax.fori_loop(0, CHIPS // BATCH, pack_signal, 0)
    wait_blocks(pairs_recv, pairs_r, BLOCKS - 1)

    def send_signal(step, carry):
        tile = chip_at(me, step)
        send_block(packed_send, packed_recv, (packed_s, packed_r), me, 2 * tile)
        send_block(packed_send, packed_recv, (packed_s, packed_r), me, 2 * tile + 1)
        return carry

    lax.fori_loop(0, CHIPS, send_signal, 0)
    inner_transform(lambda j: pairs_recv[j], l_into, spec)

    def early(group, carry):
        z = outer_transform(group, l_over, spec)
        held[:, lanes(group, 128 * GROUP)] = z
        zr, zi = z[:64], z[64:]
        ur, ui = group_turned(zr), group_turned(zi)
        im = ui * zr - ur * zi
        outer_inverse(
            group, zr * ur + zi * ui, jnp.where(group_lanes(), im, -im), l_back, spec_b
        )
        return carry

    lax.fori_loop(0, 128 // GROUP, early, 0)
    inner_inverse(l_out, spec_b, result)

    def early_out(step, carry):
        tile = chip_at(me, step)
        for j in (2 * tile, 2 * tile + 1):
            later = result[jnp.minimum(j + 1, BLOCKS - 1), 128:]
            value = result[j, 0:128] - jnp.where(j < BLOCKS - 1, later, 0.0)
            adjoint_send[j] = jnp.where(left((64, 128)), value[:64], value[64:]).astype(BF16)
            send_block(adjoint_send, adjoint_recv, (adjoint_s, adjoint_r), me, j)
        return carry

    lax.fori_loop(0, CHIPS, early_out, 0)

    wait_blocks(packed_recv, packed_r, BLOCKS - 1)

    def both_halves(j):
        p = packed_recv[j].astype(F32)
        r = turned(p)
        side = left((64, 128))
        return jnp.concatenate([jnp.where(side, p, r), jnp.where(side, r, p)], axis=0).astype(BF16)

    inner_transform(both_halves, l_into, spec)

    def late(group, carry):
        s = outer_transform(group, l_over, spec)
        z = held[:, lanes(group, 128 * GROUP)]
        zr, zi = z[:64], z[64:]
        sr, si = s[:64], s[64:]
        si = jnp.where(group_lanes(), si, -si)
        outer_inverse(group, zr * sr - zi * si, zi * sr + zr * si, l_back, spec_b)
        return carry

    lax.fori_loop(0, 128 // GROUP, late, 0)
    wait_blocks(adjoint_recv, adjoint_r, BLOCKS - 1)

    def weigh(batch, total):
        for i in range(BATCH):
            tile = batch * BATCH + i
            at = lanes(tile, 128)
            signal_adj = unpacked(adjoint_recv, tile)
            gated = qs[:, at].astype(F32) * mixed[:, at]
            kl_adj[:, at] = (signal_adj * (gated * scale * gain[:, at])).astype(BF16)
            both = signal_adj * kl[:, at].astype(F32) * gated
            gains[:, at] = jnp.sum(both * scale, axis=0, keepdims=True)
            total = total + both * gain[:, at]
        return total

    total = lax.fori_loop(0, CHIPS // BATCH, weigh, jnp.zeros((ROWS, 128), F32))
    send_sums(jnp.sum(total, axis=1, keepdims=True), inners, (inner_s, inner_r), col)
    inner_inverse(l_out, spec_b, result)

    def late_out(step, carry):
        tile = chip_at(me, step)
        for j in (2 * tile, 2 * tile + 1):
            before = jnp.where(j > 0, result[jnp.maximum(j - 1, 0), 128:], 0.0)
            later = jnp.where(j < BLOCKS - 1, result[jnp.minimum(j + 1, BLOCKS - 1), 128:], 0.0)
            value = result[j, 0:128] + jnp.where(left((ROWS, 128)), before, -later)
            joined_send[j] = value.astype(BF16)
            send_block(joined_send, joined_recv, (joined_s, joined_r), me, j)
        return carry

    lax.fori_loop(0, CHIPS, late_out, 0)

    drop = scale * scale * scale * take_sums(inners, (inner_s, inner_r)) / D

    def make_mixed_adj(batch, carry):
        for i in range(BATCH):
            tile = batch * BATCH + i
            at = lanes(tile, 128)
            q = qs[:, at].astype(F32)
            y = mixed[:, at]
            weighted = unpacked(adjoint_recv, tile) * kl[:, at].astype(F32) * gain[:, at]
            gated_adj = scale * weighted - q * y * drop
            qs_adj[:, at] = (gated_adj * y).astype(BF16)
            mixed_adj[:, at] = (gated_adj * q).astype(BF16)
        return carry

    lax.fori_loop(0, CHIPS // BATCH, make_mixed_adj, 0)
    store(0).start()
    store(3).start()

    def half_copy(tile):
        part = pl.ds(tile * (WIDE // 128), WIDE // 128)
        return neighbour_copy(
            half_send.at[part], half_recv.at[part], (half_s.at[tile], half_r.at[tile]), twin_id
        )

    def scatter(tile):
        half_copy(tile).wait_recv()
        dests = [tile * (WIDE // 128) + i for i in range(WIDE // 128)]
        for dest in dests:
            sum_send[dest] = (half_own[dest] + half_recv[dest].astype(F32)).astype(BF16)
        for dest in dests:

            @pl.when(dest != chip)
            def _():
                neighbour_copy(
                    sum_send.at[dest], sum_recv.at[chip], (sum_s, sum_r), 2 * dest + core
                ).start()

            @pl.when(dest == chip)
            def _():
                sum_recv[chip] = sum_send[chip]

    def turn(step):
        return (chip // 4 + far_first(step)) % 4

    def back_own(step, carry):
        tile = turn(step)

        @pl.when(step > 0)
        def _():
            scatter(turn(step - 1))

        at = lanes(tile, WIDE)
        m = mixed_adj[:, at]
        ms = dot(out_m[...], m)
        xs = x_hat[:, at].astype(F32)
        x_hat[:, at] = ms.astype(BF16)
        wide = m.astype(F32)
        g = rejoined(
            adjoint_product((ms[:128], ms[128:256]), (xs[:128], xs[128:256])),
            adjoint_product(
                (ms[256 : 256 + H], ms[256 + H :]), (xs[256 : 256 + H], xs[256 + H :])
            ),
        )
        zero = jnp.sum(wide * product[:, at].astype(F32), axis=0, keepdims=True)
        row = lax.broadcasted_iota(jnp.int32, (ROWS, WIDE), 0)
        part = dot(taps_t[...], g) + jnp.where(row == 0, zero, 0.0)
        gain_rows = jnp.broadcast_to(gains[:, at], (16, WIDE))
        mine = jnp.concatenate([jnp.where(core == 0, part[:64], part[64:]), gain_rows], axis=0)
        twin = jnp.concatenate([jnp.where(core == 0, part[64:], part[:64]), gain_rows], axis=0)
        for i in range(WIDE // 128):
            tile_at = slice(128 * i, 128 * (i + 1))
            half_own[tile * (WIDE // 128) + i] = mine[:, tile_at]
            half_send[tile * (WIDE // 128) + i] = twin[:, tile_at].astype(BF16)
        half_copy(tile).start()
        return carry

    lax.fori_loop(0, 2048 // WIDE, back_own, 0)
    scatter(turn(jnp.int32(2048 // WIDE - 1)))
    for tile in range(2048 // WIDE):
        after_copy(tile).start()

    wait_blocks(sum_recv, sum_r, CHIPS - 1)

    total = sum_recv[0].astype(F32)
    for j in range(1, CHIPS):
        total = total + sum_recv[j].astype(F32)
    all_half[core, chip] = total.astype(BF16)

    def gather(step, carry):
        dest = chip_at(me, step)

        @pl.when(dest != chip)
        def _():
            block = all_half.at[core, chip]
            neighbour_copy(block, block, (all_s, all_r.at[chip]), 2 * dest + core).start()

        return carry

    lax.fori_loop(0, CHIPS, gather, 0)

    def back_halo(tile, carry):
        after_copy(tile).wait_recv()
        at = lanes(tile, WIDE)
        ns = dot(next_m[...], after[:, at])
        ts, ms = f_hat[:, at].astype(F32), x_hat[256:, at].astype(F32)
        p = rejoined(
            adjoint_product((ns[:128], ns[128:]), (ts[:128], ts[128:256])),
            adjoint_product((ms[:H], ms[H:]), (ts[256 : 256 + H], ts[256 + H :])),
        )
        back = dot(into_tm[...], p) + mixed_adj[:, at].astype(F32) * fs[0:1, at].astype(F32)
        ks_adj[:, at] = (back * vs[:, at].astype(F32)).astype(BF16)
        vs_adj[:, at] = (back * ks[:, at].astype(F32)).astype(BF16)
        return carry

    lax.fori_loop(0, 2048 // WIDE, back_halo, 0)
    store(1).start()
    store(2).start()
    wait_blocks(joined_recv, joined_r, BLOCKS - 1)

    def finish(batch, carry):
        side = left((ROWS, 128))
        for i in range(BATCH):
            tile = batch * BATCH + i
            at = lanes(tile, 128)
            even, odd = joined_recv[2 * tile].astype(F32), joined_recv[2 * tile + 1].astype(F32)
            conv = jnp.where(side, even, turned(odd))
            ql_adj[:, at] = (oa[:, at].astype(F32) * conv).astype(BF16)
            fl_adj[:, at] = jnp.where(side, turned(even), odd).astype(BF16)
        return carry

    lax.fori_loop(0, CHIPS // BATCH, finish, 0)
    store(4).start()
    store(5).start()

    def forward(step, carry):
        source = chip_at(me, CHIPS - 1 - step)
        block = all_half.at[core, source]

        @pl.when(source != chip)
        def _():
            pltpu.make_async_copy(block, block, all_r.at[source]).wait()

        neighbour_copy(block, block, (twin_s, twin_r), twin_id).start()
        return carry

    lax.fori_loop(0, CHIPS, forward, 0)
    half_out = pltpu.make_async_copy(all_half.at[core], o_all.at[core], loads.at[0])
    half_out.start()
    wait_blocks(all_half.at[1 - core], twin_r, CHIPS)
    other_out = pltpu.make_async_copy(
        all_half.at[1 - core], o_all.at[1 - core], loads.at[1]
    )
    other_out.start()
    for i in range(STAGED):
        store(i).wait()
    half_out.wait()
    other_out.wait()
    wait_blocks(all_half.at[core], twin_s, CHIPS)
    for tile in range(2048 // WIDE):
        half_copy(tile).wait_send()
    for tile in range(2048 // WIDE):
        halo_copy(tile).wait_send()
        after_copy(tile).wait_send()
    wait_blocks(pairs_send, pairs_s, BLOCKS - 1)
    wait_blocks(packed_send, packed_s, BLOCKS - 1)
    wait_blocks(adjoint_send, adjoint_s, BLOCKS - 1)
    wait_blocks(joined_send, joined_s, BLOCKS - 1)
    wait_blocks(sum_send, sum_s, CHIPS - 1)
    wait_blocks(all_half.at[core], all_s, CHIPS - 1)
    wait_blocks(powers, power_s, 3)
    wait_blocks(inners, inner_s, 3)


def finish_kernel(
    sums, qs_in, ks_in, vs_in, kl_in, ql_in, fl_in,
    qs_adj, ks_adj, vs_adj, fs_adj, gain_adj, kl_adj, ql_adj, fl_adj,
):
    qs_adj[...] = qs_in[...]
    ks_adj[...] = ks_in[...]
    vs_adj[...] = vs_in[...]
    kl_adj[...] = kl_in[...]
    ql_adj[...] = ql_in[...]
    fl_adj[...] = fl_in[...]
    for tile in range(BIG // 128):
        at = slice(128 * tile, 128 * (tile + 1))
        fs_adj[0:64, at] = sums[0, tile, 0:64].astype(F32)
        fs_adj[64:128, at] = sums[1, tile, 0:64].astype(F32)
        gain_adj[:, at] = sums[0, tile, 64:80].astype(F32)[0:1]


def local(qs, ks, vs, fs, gain, kl, ql, fl, oa, contig_lengths):
    into, taps, out = (jnp.asarray(table) for table in short_tables())
    operands = [
        ks, vs, oa, ql, fl, contig_lengths[None, :], fs, into, taps, out, qs, gain[None, :], kl,
        *(jnp.asarray(table) for table in long_tables()), taps.T,
    ]
    wide = ROWS, qs.shape[1]
    row = (1, wide[1])
    table, turned_table = (1152, ROWS), (ROWS, 1152)
    full, half, sums = (BLOCKS, ROWS, 128), (BLOCKS, 64, 128), (CHIPS, 80, 128)
    spec = (BLOCKS * PITCH, 128)
    outs = [((2,) + sums, BF16)] + [(wide, BF16)] * STAGED
    scratch = [(operand.shape, operand.dtype) for operand in operands]
    scratch += [(wide, BF16)] * STAGED
    scratch += [(wide, BF16)] * 3 + [(wide, F32), (wide, BF16)]
    scratch += [((1152, wide[1]), BF16)] * 2
    scratch += [(table, BF16), (turned_table, BF16), (table, BF16), (turned_table, BF16)]
    scratch += [((256, ROWS), BF16)]
    scratch += [(full, BF16)] * 2 + [(half, BF16)] * 4 + [(full, BF16)] * 2
    scratch += [(sums, BF16)] * 2 + [(sums, F32)] + [(sums, BF16)] * 2 + [((2,) + sums, BF16)]
    scratch += [((4, 8, 128), F32)] * 2 + [(row, F32)]
    scratch += [(spec, F32)] * 2 + [((128, 128 * 128), F32), ((BLOCKS, 256, 128), F32)]
    anywhere = pl.BlockSpec(memory_space=pl.ANY)
    dma = pltpu.SemaphoreType.DMA
    shared, *staged = pl.pallas_call(
        kernel,
        out_shape=[jax.ShapeDtypeStruct(shape, dtype) for shape, dtype in outs],
        in_specs=[anywhere] * OPERANDS,
        out_specs=[anywhere] * len(outs),
        scratch_shapes=[pltpu.VMEM(shape, dtype) for shape, dtype in scratch]
        + [dma((OPERANDS,)), dma((STAGED + 1,)), *[dma((4,))] * 6, dma((CHIPS,))]
        + [dma] * 17,
        compiler_params=pltpu.CompilerParams(
            collective_id=0, has_side_effects=True, vmem_limit_bytes=62 * 1024 * 1024
        ),
    )(*operands)
    plain = pl.BlockSpec((ROWS, BIG), lambda i: (0, i))
    line = pl.BlockSpec((1, BIG), lambda i: (0, i))
    results = pl.pallas_call(
        finish_kernel,
        grid=(wide[1] // BIG,),
        out_shape=[jax.ShapeDtypeStruct(wide, BF16)] * 3
        + [jax.ShapeDtypeStruct(wide, F32), jax.ShapeDtypeStruct(row, F32)]
        + [jax.ShapeDtypeStruct(wide, BF16)] * 3,
        in_specs=[pl.BlockSpec((2, BIG // 128, 80, 128), lambda i: (0, i, 0, 0))]
        + [plain] * STAGED,
        out_specs=[plain] * 4 + [line] + [plain] * 3,
    )(shared, *staged)
    qs_adj, ks_adj, vs_adj, fs_adj, gain_adj, kl_adj, ql_adj, fl_adj = results
    return qs_adj, ks_adj, vs_adj, fs_adj, gain_adj[0], kl_adj, ql_adj, fl_adj


def solution(mesh):
    spread_spec = P("ctx", "tp")
    in_specs = (
        spread_spec, spread_spec, spread_spec, P(None, "tp"), P("tp"),
        spread_spec, spread_spec, spread_spec, spread_spec, P(),
    )
    out_specs = (
        spread_spec, spread_spec, spread_spec, P(None, "tp"), P("tp"),
        spread_spec, spread_spec, spread_spec,
    )
    return jax.shard_map(local, mesh=mesh, in_specs=in_specs, out_specs=out_specs, check_vma=False)
```

```python
import math

import jax
import jax.numpy as jnp
import ml_dtypes
import numpy as np
from jax import lax
from jax.experimental import pallas as pl
from jax.experimental.pallas import tpu as pltpu
from jax.sharding import PartitionSpec as P

D = 8192
EPS = 1e-06
F32 = jnp.float32
BF16 = jnp.bfloat16
ROWS = 128
BLOCKS = 32
HALVES = (64, 32, 16, 8, 4, 2, 1)
PITCH = 264
VMEM = pl.BlockSpec(memory_space=pltpu.VMEM)


def odd_angles(size):
    return 2.0 * math.pi * (np.arange(size // 2) + 0.5) / size


def short_tables():
    into_re, into_im, taps_re, taps_im, out_re, out_im = ([] for _ in range(6))
    for half in (ROWS,) + HALVES:
        theta = odd_angles(2 * half)
        pairs = 1 if half == ROWS else ROWS // (2 * half)
        for pair in range(pairs):
            base = 0 if half == ROWS else pair * 2 * half
            first = np.zeros((half, ROWS)), np.zeros((half, ROWS))
            last = np.zeros((half, ROWS)), np.zeros((half, ROWS))
            taps = np.zeros((half, ROWS)), np.zeros((half, ROWS))
            ramp = np.arange(half)
            first[0][:, base : base + half] = np.cos(np.outer(theta, ramp))
            first[1][:, base : base + half] = -np.sin(np.outer(theta, ramp))
            start = 0 if half == ROWS else base + half
            last[0][:, start : start + half] = np.cos(np.outer(theta, ramp + half)) / half
            last[1][:, start : start + half] = -np.sin(np.outer(theta, ramp + half)) / half
            lags = np.arange(1, min(2 * half, ROWS))
            taps[0][:, lags] = np.cos(np.outer(theta, lags))
            taps[1][:, lags] = -np.sin(np.outer(theta, lags))
            for parts, pair_of in ((into_re, first), (out_re, last), (taps_re, taps)):
                parts.append(pair_of[0])
            for parts, pair_of in ((into_im, first), (out_im, last), (taps_im, taps)):
                parts.append(pair_of[1])

    def joined(re, im):
        re, im = np.concatenate(re), np.concatenate(im)
        return np.concatenate([re[:ROWS], im[:ROWS], re[ROWS:], im[ROWS:]]).astype(ml_dtypes.bfloat16)

    return joined(into_re, into_im), joined(taps_re, taps_im), joined(out_re, out_im)


def long_tables():
    theta = odd_angles(256)
    inner = np.outer(theta, np.arange(ROWS))
    into = np.concatenate([np.cos(inner), -np.sin(inner)])
    outer = np.outer(np.arange(256), theta)
    out = np.concatenate([np.cos(outer), -np.sin(outer)], axis=1) / 128.0
    angle = 2.0 * math.pi * (np.outer(np.arange(64), np.arange(BLOCKS)) % 64) / 64.0
    cos, sin = np.cos(angle), np.sin(angle)
    over = np.block([[cos, sin], [-sin, cos]])
    back = np.block([[cos.T, -sin.T], [sin.T, cos.T]]) / 64.0
    halves = np.concatenate([np.arange(64), np.arange(128, 192)])
    paired = out[:, np.concatenate([halves, halves + 64])]
    return [table.astype(ml_dtypes.bfloat16) for table in (into, over, back, out, paired)]


def dot(a, b):
    return jnp.dot(a, b, preferred_element_type=F32)


def turned(x):
    return pltpu.roll(x, 64, 1)


def left(shape):
    return lax.broadcasted_iota(jnp.int32, shape, 1) < 64


def lanes(tile, width):
    return pl.ds(pl.multiple_of(tile * width, width), width)


def mask_rows(lengths, first):
    before = lax.broadcasted_iota(jnp.int32, (64, 64), 1) < lax.broadcasted_iota(
        jnp.int32, (64, 64), 0
    )
    starts = jnp.sum(jnp.where(before, lengths, 0), axis=1, keepdims=True)
    tokens = BLOCKS * ROWS

    def label(positions):
        place = positions + first
        begun = jnp.sum(jnp.where(place >= starts, 1, 0), axis=0, keepdims=True)
        return begun + jnp.where(place >= tokens, 1, 0)

    own = lax.broadcasted_iota(jnp.int32, (1, ROWS), 1)
    here = label(own)
    before_here = label(own - own - 1)
    last_here = label(own - own + (ROWS - 1))

    def same(a, b):
        return (a == b).astype(F32)

    halves = [same(here, label((own // (2 * half)) * (2 * half) + half - 1)) for half in HALVES]
    return dict(
        halves=halves,
        halo_own=same(here, before_here),
        halo_before=same(label(own - ROWS), before_here),
        next_own=same(here, last_here),
        next_after=same(label(own + ROWS), last_here),
    )


def spread(masks, head):
    parts = [jnp.broadcast_to(masks[head], (256, ROWS))]
    for _ in range(2):
        parts += [jnp.broadcast_to(mask, (64, ROWS)) for mask in masks["halves"]]
    return jnp.concatenate(parts, axis=0)


def masked(table, masks, head):
    return (table.astype(F32) * spread(masks, head)).astype(BF16)


H = 448


def complex_product(a, b):
    return a[0] * b[0] - a[1] * b[1], a[0] * b[1] + a[1] * b[0]


def adjoint_product(a, b):
    return a[0] * b[0] + a[1] * b[1], a[1] * b[0] - a[0] * b[1]


def split_spectrum(table, head_rows, body_rows):
    head = dot(table[0:256, :], head_rows)
    body = dot(table[256:, :], body_rows)
    return (head[:128], head[128:]), (body[:H], body[H:])


def rejoined(head, body):
    return jnp.concatenate([head[0], head[1], body[0], body[1]], axis=0).astype(BF16)


GROUP = 16
SPAN = 8
WIDE = 512
BIG = 1024
CHIPS = 16
MESH = pl.DeviceIdType.MESH


def inner_transform(read, into, spec):
    def step(j, carry):
        value = dot(into[...], jnp.concatenate([read(SPAN * j + i) for i in range(SPAN)], axis=1))
        for i in range(SPAN):
            spec[pl.ds((SPAN * j + i) * PITCH, 256), :] = value[:, 128 * i : 128 * (i + 1)]
        return carry

    lax.fori_loop(0, BLOCKS // SPAN, step, 0)


def place(group, member):
    return group * (GROUP // 2) + member % (GROUP // 2) + 64 * (member // (GROUP // 2))


def outer_transform(group, over, spec):
    columns = []
    for member in range(GROUP):
        f = place(group, member)
        columns.append(
            jnp.concatenate(
                [
                    spec[pl.ds(f, BLOCKS, stride=PITCH), :],
                    spec[pl.ds(f + 128, BLOCKS, stride=PITCH), :],
                ],
                axis=0,
            )
        )
    return dot(over[...], jnp.concatenate(columns, axis=1).astype(BF16))


def outer_inverse(group, re, im, back, spec):
    result = dot(back[...], jnp.concatenate([re, im], axis=0).astype(BF16))
    for member in range(GROUP):
        f = place(group, member)
        piece = result[:, 128 * member : 128 * (member + 1)]
        spec[pl.ds(f, BLOCKS, stride=PITCH), :] = piece[:BLOCKS]
        spec[pl.ds(f + 128, BLOCKS, stride=PITCH), :] = piece[BLOCKS:]


def inner_inverse(out, spec, result):
    def step(j, carry):
        value = dot(
            out[...],
            jnp.concatenate(
                [spec[pl.ds((SPAN * j + i) * PITCH, 256), :].astype(BF16) for i in range(SPAN)],
                axis=1,
            ),
        )
        for i in range(SPAN):
            result[SPAN * j + i] = value[:, 128 * i : 128 * (i + 1)]
        return carry

    lax.fori_loop(0, BLOCKS // SPAN, step, 0)


def group_lanes(members):
    return (lax.broadcasted_iota(jnp.int32, (64, 128 * members), 1) & 127) < 64


def group_turned(x, members):
    return jnp.concatenate(
        [turned(x[:, 128 * m : 128 * (m + 1)]) for m in range(members)], axis=1
    )


def paired_spectra(x):
    members = GROUP // 2
    low, high = x[:, : 128 * members], x[:, 128 * members :]
    side = group_lanes(members)
    return (
        jnp.where(side, low, group_turned(high, members)),
        jnp.where(side, group_turned(low, members), high),
    )


def paired_inverse(out, spec, result):
    def step(quad, carry):
        columns = []
        for i in range(4):
            first = spec[pl.ds((8 * quad + 2 * i) * PITCH, 128), :]
            second = spec[pl.ds((8 * quad + 2 * i + 1) * PITCH, 128), :]
            side = left((128, 128))
            columns.append(
                jnp.concatenate(
                    [
                        jnp.where(side, first, turned(second)),
                        jnp.where(side, turned(first), second),
                    ],
                    axis=0,
                )
            )
        value = dot(out[...], jnp.concatenate(columns, axis=1).astype(BF16))
        for i in range(4):
            result[4 * quad + i] = value[:, 128 * i : 128 * (i + 1)]
        return carry

    lax.fori_loop(0, 4, step, 0)


def unpacked(adjoint, tile):
    even, odd = adjoint[2 * tile].astype(F32), adjoint[2 * tile + 1].astype(F32)
    side = left((64, 128))
    return jnp.concatenate(
        [jnp.where(side, even, turned(odd)), jnp.where(side, turned(even), odd)], axis=0
    )


def far_first(step):
    return jnp.where(step == 0, 2, jnp.where(step == 1, 1, jnp.where(step == 2, 3, 0)))


def chip_at(me, step):
    chip = me // 2
    return (chip // 4 + far_first(step // 4)) % 4 * 4 + (chip % 4 + far_first(step % 4)) % 4


def send_block(send, recv, sems, me, dest):
    @pl.when(dest != me)
    def _():
        pltpu.make_async_remote_copy(
            src_ref=send.at[dest],
            dst_ref=recv.at[me],
            send_sem=sems[0],
            recv_sem=sems[1],
            device_id={"ctx": dest},
            device_id_type=MESH,
        ).start()

    @pl.when(dest == me)
    def _():
        recv[me] = send[me]


def wait_blocks(buffer, sem, count):
    part = buffer.at[pl.ds(0, count)]
    pltpu.make_async_copy(part, part, sem).wait()


def neighbour_copy(source, target, sems, dest):
    return pltpu.make_async_remote_copy(
        src_ref=source,
        dst_ref=target,
        send_sem=sems[0],
        recv_sem=sems[1],
        device_id={"ctx": dest},
        device_id_type=MESH,
    )


def send_sums(column, buffer, sems, col):
    buffer[col] = jnp.broadcast_to(column, (ROWS, 128)).T[:8]
    for step in range(1, 4):
        pltpu.make_async_remote_copy(
            src_ref=buffer.at[col],
            dst_ref=buffer.at[col],
            send_sem=sems[0],
            recv_sem=sems[1],
            device_id={"tp": (col + step) % 4},
            device_id_type=MESH,
        ).start()


def take_sums(buffer, sems):
    wait_blocks(buffer, sems[1], 3)
    row = buffer[0, 0:1] + buffer[1, 0:1] + buffer[2, 0:1] + buffer[3, 0:1]
    return jnp.broadcast_to(row, (ROWS, 128)).T


OPERANDS = 19
STAGED = 6
BATCH = 4


def kernel(*refs):
    far = refs[:OPERANDS]
    o_all, *o_staged = refs[OPERANDS : OPERANDS + 1 + STAGED]
    near = refs[OPERANDS + 1 + STAGED : 2 * OPERANDS + 1 + STAGED]
    (
        qs_adj, ks_adj, vs_adj, kl_adj, ql_adj, fl_adj,
        product, halo, after, mixed, mixed_adj, x_hat, f_hat,
        into_m, into_tm, out_m, out_tm, next_m,
        pairs_send, pairs_recv, packed_send, packed_recv, adjoint_send, adjoint_recv,
        joined_send, joined_recv, half_send, half_recv, half_own, sum_send, sum_recv, all_half,
        powers, inners, gains, spec, spec_b, held, result,
        loads, stores, half_s, half_r, halo_s, halo_r, after_s, after_r, all_r,
        pairs_s, pairs_r, packed_s, packed_r, adjoint_s, adjoint_r, joined_s, joined_r,
        sum_s, sum_r, all_s,
        power_s, power_r, inner_s, inner_r, twin_s, twin_r,
    ) = refs[2 * OPERANDS + 1 + STAGED :]
    (
        ks, vs, oa, ql, fl, lengths, fs, into, taps, out, qs, gain, kl, l_into, l_over,
        l_back, l_out, l_pair, taps_t,
    ) = near

    def load(i):
        return pltpu.make_async_copy(far[i], near[i], loads.at[i])

    def store(i):
        source = (qs_adj, ks_adj, vs_adj, kl_adj, ql_adj, fl_adj)[i]
        return pltpu.make_async_copy(source, o_staged[i], stores.at[i])

    me, col = lax.axis_index("ctx"), lax.axis_index("tp")
    chip, core = me // 2, me % 2
    twin_id = 2 * chip + 1 - core
    barrier = pltpu.get_barrier_semaphore()
    for i in range(OPERANDS):
        load(i).start()

    def greet(step, carry):
        pl.semaphore_signal(
            barrier, inc=1, device_id={"ctx": (me + step) % BLOCKS}, device_id_type=MESH
        )
        return carry

    lax.fori_loop(1, BLOCKS, greet, 0)
    for step in range(1, 4):
        pl.semaphore_signal(
            barrier, inc=1, device_id={"tp": (col + step) % 4}, device_id_type=MESH
        )

    load(0).wait()
    load(1).wait()

    def make_product(tile, carry):
        at = lanes(tile, WIDE)
        product[:, at] = (ks[:, at].astype(F32) * vs[:, at].astype(F32)).astype(BF16)
        return carry

    lax.fori_loop(0, 2048 // WIDE, make_product, 0)
    pl.semaphore_wait(barrier, BLOCKS - 1 + 3)

    def halo_copy(tile):
        part = product.at[:, lanes(tile, WIDE)], halo.at[:, lanes(tile, WIDE)]
        return neighbour_copy(*part, (halo_s.at[tile], halo_r.at[tile]), (me + 1) % BLOCKS)

    def after_copy(tile):
        part = mixed_adj.at[:, lanes(tile, WIDE)], after.at[:, lanes(tile, WIDE)]
        dest = (me + BLOCKS - 1) % BLOCKS
        return neighbour_copy(*part, (after_s.at[tile], after_r.at[tile]), dest)

    for tile in range(2048 // WIDE):
        halo_copy(tile).start()
    for i in range(2, 5):
        load(i).wait()

    def pack_pairs(batch, carry):
        deep = (chip % 4 + 4 - batch) % 4
        tiles = [(chip // 4 + i) % 4 * 4 + deep for i in (2, 1, 3, 0)]
        side = left((ROWS, 128))
        for tile in tiles:
            at = lanes(tile, 128)
            up = (oa[:, at].astype(F32) * ql[:, at].astype(F32)).astype(BF16).astype(F32)
            lags = fl[:, at].astype(F32)
            pairs_send[2 * tile] = jnp.where(side, lags, turned(up)).astype(BF16)
            pairs_send[2 * tile + 1] = jnp.where(side, turned(lags), up).astype(BF16)
        for tile in tiles:
            send_block(pairs_send, pairs_recv, (pairs_s, pairs_r), me, 2 * tile)
            send_block(pairs_send, pairs_recv, (pairs_s, pairs_r), me, 2 * tile + 1)
        return carry

    lax.fori_loop(0, 1, pack_pairs, 0)

    for i in range(5, OPERANDS):
        load(i).wait()
    masks = mask_rows(lengths[...], me * ROWS)
    into_m[...] = masked(into[...], masks, "halo_before")
    into_tm[...] = masked(into[...], masks, "next_own").astype(F32).T.astype(BF16)
    out_m[...] = masked(out[...], masks, "halo_own")
    out_tm[...] = out_m[...].astype(F32).T.astype(BF16)
    next_m[...] = (out[0:256, :].astype(F32) * masks["next_after"]).astype(BF16)

    def short_own(tile, carry):
        at = lanes(tile, WIDE)
        x, f = product[:, at], fs[:, at]
        xs, ts = dot(into_m[256:, :], x), dot(taps[...], f)
        x_hat[256:, at] = xs.astype(BF16)
        f_hat[:, at] = ts.astype(BF16)
        re, im = complex_product((xs[:H], xs[H:]), (ts[256 : 256 + H], ts[256 + H :]))
        q = jnp.concatenate([re, im], axis=0).astype(BF16)
        mixed[:, at] = dot(out_tm[:, 256:], q) + x.astype(F32) * f[0:1, :].astype(F32)
        return carry

    lax.fori_loop(0, 2048 // WIDE, short_own, 0)
    for tile in range(2048 // WIDE):
        halo_copy(tile).wait_recv()
    lax.fori_loop(1, CHIPS // BATCH, pack_pairs, 0)

    def short_halo(tile, total):
        at = lanes(tile, WIDE)
        xs = dot(into_m[0:256, :], halo[:, at])
        x_hat[0:256, at] = xs.astype(BF16)
        ts = f_hat[0:256, at].astype(F32)
        re, im = complex_product((xs[:128], xs[128:]), (ts[:128], ts[128:]))
        q = jnp.concatenate([re, im], axis=0).astype(BF16)
        y = mixed[:, at] + dot(out_tm[:, 0:256], q)
        mixed[:, at] = y
        gated = qs[:, at].astype(F32) * y
        return total + jnp.sum(gated * gated, axis=1, keepdims=True)

    total = lax.fori_loop(0, 2048 // WIDE, short_halo, jnp.zeros((ROWS, 1), F32))
    send_sums(total, powers, (power_s, power_r), col)

    scale = lax.rsqrt(take_sums(powers, (power_s, power_r)) / D + EPS)

    def pack_signal(batch, carry):
        tiles = [batch * BATCH + i for i in range(BATCH)]
        side = left((64, 128))
        for tile in tiles:
            at = lanes(tile, 128)
            gated = qs[:, at].astype(F32) * mixed[:, at]
            s = gated * scale * gain[:, at] * kl[:, at].astype(F32)
            low, high = s[:64], s[64:]
            packed_send[2 * tile] = jnp.where(side, low, turned(high)).astype(BF16)
            packed_send[2 * tile + 1] = jnp.where(side, turned(low), high).astype(BF16)
        return carry

    lax.fori_loop(0, CHIPS // BATCH, pack_signal, 0)
    wait_blocks(pairs_recv, pairs_r, BLOCKS - 1)

    def send_signal(step, carry):
        tile = chip_at(me, step)
        send_block(packed_send, packed_recv, (packed_s, packed_r), me, 2 * tile)
        send_block(packed_send, packed_recv, (packed_s, packed_r), me, 2 * tile + 1)
        return carry

    lax.fori_loop(0, CHIPS, send_signal, 0)
    inner_transform(lambda j: pairs_recv[j], l_into, spec)

    def early(group, carry):
        z = outer_transform(group, l_over, spec)
        held[:, lanes(group, 128 * GROUP)] = z
        fr, ur = paired_spectra(z[:64])
        fi, ui = paired_spectra(z[64:])
        both = jnp.concatenate([fr * ur + fi * ui, ui * fr - ur * fi], axis=0).astype(BF16)
        value = dot(l_back[...], both)
        for member in range(GROUP // 2):
            f = group * (GROUP // 2) + member
            piece = value[:, 128 * member : 128 * (member + 1)]
            spec_b[pl.ds(f, BLOCKS, stride=PITCH), :] = piece[:BLOCKS]
            spec_b[pl.ds(f + 64, BLOCKS, stride=PITCH), :] = piece[BLOCKS:]
        return carry

    lax.fori_loop(0, 128 // GROUP, early, 0)
    paired_inverse(l_pair, spec_b, result)

    def early_out(step, carry):
        tile = chip_at(me, step)
        later = jnp.where(tile < CHIPS - 1, result[jnp.minimum(tile + 1, CHIPS - 1), 128:], 0.0)
        tail = turned(jnp.where(left((ROWS, 128)), later, result[tile, 128:]))
        value = result[tile, 0:128] - tail
        low, high = value[:64], value[64:]
        side = left((64, 128))
        adjoint_send[2 * tile] = jnp.where(side, low, turned(high)).astype(BF16)
        adjoint_send[2 * tile + 1] = jnp.where(side, turned(low), high).astype(BF16)
        for j in (2 * tile, 2 * tile + 1):
            send_block(adjoint_send, adjoint_recv, (adjoint_s, adjoint_r), me, j)
        return carry

    lax.fori_loop(0, CHIPS, early_out, 0)

    wait_blocks(packed_recv, packed_r, BLOCKS - 1)

    def both_halves(j):
        p = packed_recv[j].astype(F32)
        r = turned(p)
        side = left((64, 128))
        return jnp.concatenate([jnp.where(side, p, r), jnp.where(side, r, p)], axis=0).astype(BF16)

    inner_transform(both_halves, l_into, spec)

    def late(group, carry):
        s = outer_transform(group, l_over, spec)
        z = held[:, lanes(group, 128 * GROUP)]
        zr, zi = z[:64], z[64:]
        sr, si = s[:64], s[64:]
        si = jnp.where(group_lanes(GROUP), si, -si)
        outer_inverse(group, zr * sr - zi * si, zi * sr + zr * si, l_back, spec_b)
        return carry

    lax.fori_loop(0, 128 // GROUP, late, 0)
    wait_blocks(adjoint_recv, adjoint_r, BLOCKS - 1)

    def weigh(batch, total):
        for i in range(BATCH):
            tile = batch * BATCH + i
            at = lanes(tile, 128)
            signal_adj = unpacked(adjoint_recv, tile)
            gated = qs[:, at].astype(F32) * mixed[:, at]
            kl_adj[:, at] = (signal_adj * (gated * scale * gain[:, at])).astype(BF16)
            both = signal_adj * kl[:, at].astype(F32) * gated
            gains[:, at] = jnp.sum(both * scale, axis=0, keepdims=True)
            total = total + both * gain[:, at]
        return total

    total = lax.fori_loop(0, CHIPS // BATCH, weigh, jnp.zeros((ROWS, 128), F32))
    send_sums(jnp.sum(total, axis=1, keepdims=True), inners, (inner_s, inner_r), col)
    inner_inverse(l_out, spec_b, result)

    def late_out(step, carry):
        tile = chip_at(me, step)
        for j in (2 * tile, 2 * tile + 1):
            before = jnp.where(j > 0, result[jnp.maximum(j - 1, 0), 128:], 0.0)
            later = jnp.where(j < BLOCKS - 1, result[jnp.minimum(j + 1, BLOCKS - 1), 128:], 0.0)
            value = result[j, 0:128] + jnp.where(left((ROWS, 128)), before, -later)
            joined_send[j] = value.astype(BF16)
            send_block(joined_send, joined_recv, (joined_s, joined_r), me, j)
        return carry

    lax.fori_loop(0, CHIPS, late_out, 0)

    drop = scale * scale * scale * take_sums(inners, (inner_s, inner_r)) / D

    def make_mixed_adj(batch, carry):
        for i in range(BATCH):
            tile = batch * BATCH + i
            at = lanes(tile, 128)
            q = qs[:, at].astype(F32)
            y = mixed[:, at]
            weighted = unpacked(adjoint_recv, tile) * kl[:, at].astype(F32) * gain[:, at]
            gated_adj = scale * weighted - q * y * drop
            qs_adj[:, at] = (gated_adj * y).astype(BF16)
            mixed_adj[:, at] = (gated_adj * q).astype(BF16)
        return carry

    lax.fori_loop(0, CHIPS // BATCH, make_mixed_adj, 0)
    store(0).start()
    store(3).start()

    def half_copy(tile):
        part = pl.ds(tile * (WIDE // 128), WIDE // 128)
        return neighbour_copy(
            half_send.at[part], half_recv.at[part], (half_s.at[tile], half_r.at[tile]), twin_id
        )

    def scatter(tile):
        half_copy(tile).wait_recv()
        dests = [tile * (WIDE // 128) + i for i in range(WIDE // 128)]
        for dest in dests:
            sum_send[dest] = (half_own[dest] + half_recv[dest].astype(F32)).astype(BF16)
        for dest in dests:

            @pl.when(dest != chip)
            def _():
                neighbour_copy(
                    sum_send.at[dest], sum_recv.at[chip], (sum_s, sum_r), 2 * dest + core
                ).start()

            @pl.when(dest == chip)
            def _():
                sum_recv[chip] = sum_send[chip]

    def turn(step):
        return (chip // 4 + far_first(step)) % 4

    def back_own(step, carry):
        tile = turn(step)

        at = lanes(tile, WIDE)
        m = mixed_adj[:, at]
        ms = dot(out_m[...], m)
        xs = x_hat[:, at].astype(F32)
        x_hat[:, at] = ms.astype(BF16)
        wide = m.astype(F32)
        g = rejoined(
            adjoint_product((ms[:128], ms[128:256]), (xs[:128], xs[128:256])),
            adjoint_product(
                (ms[256 : 256 + H], ms[256 + H :]), (xs[256 : 256 + H], xs[256 + H :])
            ),
        )
        zero = jnp.sum(wide * product[:, at].astype(F32), axis=0, keepdims=True)
        row = lax.broadcasted_iota(jnp.int32, (ROWS, WIDE), 0)
        part = dot(taps_t[...], g) + jnp.where(row == 0, zero, 0.0)
        gain_rows = jnp.broadcast_to(gains[:, at], (16, WIDE))
        mine = jnp.concatenate([jnp.where(core == 0, part[:64], part[64:]), gain_rows], axis=0)
        twin = jnp.concatenate([jnp.where(core == 0, part[64:], part[:64]), gain_rows], axis=0)
        for i in range(WIDE // 128):
            tile_at = slice(128 * i, 128 * (i + 1))
            half_own[tile * (WIDE // 128) + i] = mine[:, tile_at]
            half_send[tile * (WIDE // 128) + i] = twin[:, tile_at].astype(BF16)
        half_copy(tile).start()
        return carry

    lax.fori_loop(0, 2048 // WIDE, back_own, 0)
    for step in range(2048 // WIDE):
        scatter(turn(jnp.int32(step)))
    for tile in range(2048 // WIDE):
        after_copy(tile).start()

    wait_blocks(sum_recv, sum_r, CHIPS - 1)

    total = sum_recv[0].astype(F32)
    for j in range(1, CHIPS):
        total = total + sum_recv[j].astype(F32)
    all_half[core, chip] = total.astype(BF16)

    def gather(step, carry):
        dest = chip_at(me, step)

        @pl.when(dest != chip)
        def _():
            block = all_half.at[core, chip]
            neighbour_copy(block, block, (all_s, all_r.at[chip]), 2 * dest + core).start()

        return carry

    lax.fori_loop(0, CHIPS, gather, 0)

    def back_halo(tile, carry):
        after_copy(tile).wait_recv()
        at = lanes(tile, WIDE)
        ns = dot(next_m[...], after[:, at])
        ts, ms = f_hat[:, at].astype(F32), x_hat[256:, at].astype(F32)
        p = rejoined(
            adjoint_product((ns[:128], ns[128:]), (ts[:128], ts[128:256])),
            adjoint_product((ms[:H], ms[H:]), (ts[256 : 256 + H], ts[256 + H :])),
        )
        back = dot(into_tm[...], p) + mixed_adj[:, at].astype(F32) * fs[0:1, at].astype(F32)
        ks_adj[:, at] = (back * vs[:, at].astype(F32)).astype(BF16)
        vs_adj[:, at] = (back * ks[:, at].astype(F32)).astype(BF16)
        return carry

    lax.fori_loop(0, 2048 // WIDE, back_halo, 0)
    store(1).start()
    store(2).start()
    wait_blocks(joined_recv, joined_r, BLOCKS - 1)

    def finish(batch, carry):
        side = left((ROWS, 128))
        for i in range(BATCH):
            tile = batch * BATCH + i
            at = lanes(tile, 128)
            even, odd = joined_recv[2 * tile].astype(F32), joined_recv[2 * tile + 1].astype(F32)
            conv = jnp.where(side, even, turned(odd))
            ql_adj[:, at] = (oa[:, at].astype(F32) * conv).astype(BF16)
            fl_adj[:, at] = jnp.where(side, turned(even), odd).astype(BF16)
        return carry

    lax.fori_loop(0, CHIPS // BATCH, finish, 0)
    store(4).start()
    store(5).start()

    def forward(step, carry):
        source = chip_at(me, CHIPS - 1 - step)
        block = all_half.at[core, source]

        @pl.when(source != chip)
        def _():
            pltpu.make_async_copy(block, block, all_r.at[source]).wait()

        neighbour_copy(block, block, (twin_s, twin_r), twin_id).start()
        return carry

    lax.fori_loop(0, CHIPS, forward, 0)
    half_out = pltpu.make_async_copy(all_half.at[core], o_all.at[core], loads.at[0])
    half_out.start()
    wait_blocks(all_half.at[1 - core], twin_r, CHIPS)
    other_out = pltpu.make_async_copy(
        all_half.at[1 - core], o_all.at[1 - core], loads.at[1]
    )
    other_out.start()
    for i in range(STAGED):
        store(i).wait()
    half_out.wait()
    other_out.wait()
    wait_blocks(all_half.at[core], twin_s, CHIPS)
    for tile in range(2048 // WIDE):
        half_copy(tile).wait_send()
    for tile in range(2048 // WIDE):
        halo_copy(tile).wait_send()
        after_copy(tile).wait_send()
    wait_blocks(pairs_send, pairs_s, BLOCKS - 1)
    wait_blocks(packed_send, packed_s, BLOCKS - 1)
    wait_blocks(adjoint_send, adjoint_s, BLOCKS - 1)
    wait_blocks(joined_send, joined_s, BLOCKS - 1)
    wait_blocks(sum_send, sum_s, CHIPS - 1)
    wait_blocks(all_half.at[core], all_s, CHIPS - 1)
    wait_blocks(powers, power_s, 3)
    wait_blocks(inners, inner_s, 3)


def finish_kernel(
    sums, qs_in, ks_in, vs_in, kl_in, ql_in, fl_in,
    qs_adj, ks_adj, vs_adj, fs_adj, gain_adj, kl_adj, ql_adj, fl_adj,
):
    qs_adj[...] = qs_in[...]
    ks_adj[...] = ks_in[...]
    vs_adj[...] = vs_in[...]
    kl_adj[...] = kl_in[...]
    ql_adj[...] = ql_in[...]
    fl_adj[...] = fl_in[...]
    for tile in range(BIG // 128):
        at = slice(128 * tile, 128 * (tile + 1))
        fs_adj[0:64, at] = sums[0, tile, 0:64].astype(F32)
        fs_adj[64:128, at] = sums[1, tile, 0:64].astype(F32)
        gain_adj[:, at] = sums[0, tile, 64:80].astype(F32)[0:1]


def local(qs, ks, vs, fs, gain, kl, ql, fl, oa, contig_lengths):
    into, taps, out = (jnp.asarray(table) for table in short_tables())
    operands = [
        ks, vs, oa, ql, fl, contig_lengths[None, :], fs, into, taps, out, qs, gain[None, :], kl,
        *(jnp.asarray(table) for table in long_tables()), taps.T,
    ]
    wide = ROWS, qs.shape[1]
    row = (1, wide[1])
    table, turned_table = (1152, ROWS), (ROWS, 1152)
    full, half, sums = (BLOCKS, ROWS, 128), (BLOCKS, 64, 128), (CHIPS, 80, 128)
    spec = (BLOCKS * PITCH, 128)
    outs = [((2,) + sums, BF16)] + [(wide, BF16)] * STAGED
    scratch = [(operand.shape, operand.dtype) for operand in operands]
    scratch += [(wide, BF16)] * STAGED
    scratch += [(wide, BF16)] * 3 + [(wide, F32), (wide, BF16)]
    scratch += [((1152, wide[1]), BF16)] * 2
    scratch += [(table, BF16), (turned_table, BF16), (table, BF16), (turned_table, BF16)]
    scratch += [((256, ROWS), BF16)]
    scratch += [(full, BF16)] * 2 + [(half, BF16)] * 4 + [(full, BF16)] * 2
    scratch += [(sums, BF16)] * 2 + [(sums, F32)] + [(sums, BF16)] * 2 + [((2,) + sums, BF16)]
    scratch += [((4, 8, 128), F32)] * 2 + [(row, F32)]
    scratch += [(spec, F32)] * 2 + [((128, 128 * 128), F32), ((BLOCKS, 256, 128), F32)]
    anywhere = pl.BlockSpec(memory_space=pl.ANY)
    dma = pltpu.SemaphoreType.DMA
    shared, *staged = pl.pallas_call(
        kernel,
        out_shape=[jax.ShapeDtypeStruct(shape, dtype) for shape, dtype in outs],
        in_specs=[anywhere] * OPERANDS,
        out_specs=[anywhere] * len(outs),
        scratch_shapes=[pltpu.VMEM(shape, dtype) for shape, dtype in scratch]
        + [dma((OPERANDS,)), dma((STAGED + 1,)), *[dma((4,))] * 6, dma((CHIPS,))]
        + [dma] * 17,
        compiler_params=pltpu.CompilerParams(
            collective_id=0, has_side_effects=True, vmem_limit_bytes=62 * 1024 * 1024
        ),
    )(*operands)
    plain = pl.BlockSpec((ROWS, BIG), lambda i: (0, i))
    line = pl.BlockSpec((1, BIG), lambda i: (0, i))
    results = pl.pallas_call(
        finish_kernel,
        grid=(wide[1] // BIG,),
        out_shape=[jax.ShapeDtypeStruct(wide, BF16)] * 3
        + [jax.ShapeDtypeStruct(wide, F32), jax.ShapeDtypeStruct(row, F32)]
        + [jax.ShapeDtypeStruct(wide, BF16)] * 3,
        in_specs=[pl.BlockSpec((2, BIG // 128, 80, 128), lambda i: (0, i, 0, 0))]
        + [plain] * STAGED,
        out_specs=[plain] * 4 + [line] + [plain] * 3,
    )(shared, *staged)
    qs_adj, ks_adj, vs_adj, fs_adj, gain_adj, kl_adj, ql_adj, fl_adj = results
    return qs_adj, ks_adj, vs_adj, fs_adj, gain_adj[0], kl_adj, ql_adj, fl_adj


def solution(mesh):
    spread_spec = P("ctx", "tp")
    in_specs = (
        spread_spec, spread_spec, spread_spec, P(None, "tp"), P("tp"),
        spread_spec, spread_spec, spread_spec, spread_spec, P(),
    )
    out_specs = (
        spread_spec, spread_spec, spread_spec, P(None, "tp"), P("tp"),
        spread_spec, spread_spec, spread_spec,
    )
    return jax.shard_map(local, mesh=mesh, in_specs=in_specs, out_specs=out_specs, check_vma=False)
```
